256 devices in a mesh: section: 16 (over z, core), mp: 8 (over x_lo, y), dp: 2 (over x_hi).
Axes of the slice: x: 4 (x_hi: 2, x_lo: 2; x = x_hi * 2 + x_lo), y: 4, z: 8, core: 2. Of those that a mesh axis runs over, the one named last changes fastest.
Arguments:
- arriving: bfloat16 [16, 256, 4096], P('section', 'dp', 'mp'), may hold values from -6 to 6
- returning: bfloat16 [16, 256, 4096], P('section', 'dp', 'mp'), may hold values from -6 to 6
- entering: bfloat16 [2, 256, 4096], P(None, 'dp', 'mp'), may hold values from -6 to 6
- cot_entering: bfloat16 [2, 256, 4096], P(None, 'dp', 'mp'), may hold values from -6 to 6
- home_stash: bfloat16 [16, 3, 256, 4096], P('section', None, 'dp', 'mp'), may hold values from -6 to 6
- spare_stash: bfloat16 [16, 3, 256, 4096], P('section', None, 'dp', 'mp'), may hold values from -6 to 6
- evicted: int32 [16, 3], P('section'), may hold values from 0 to 1, as said below
- norm_gain: float32 [16, 4096], P('section'), may hold values from 0.25 to 1.75
- query_weight_matrix: bfloat16 [16, 4096, 4096], P('section', None, 'mp'), may hold values from -1 to 1
- key_weight_matrix: bfloat16 [16, 4096, 1024], P('section', None, 'mp'), may hold values from -1 to 1
- value_weight_matrix: bfloat16 [16, 4096, 1024], P('section', None, 'mp'), may hold values from -0.09375 to 0.09375
- w_output: bfloat16 [16, 4096, 4096], P('section', 'mp'), may hold values from -0.09375 to 0.09375
Outputs:
- section_outputs: bfloat16 [16, 3, 256, 4096], P('section', None, 'dp', 'mp')
- section_cotangents: bfloat16 [16, 3, 256, 4096], P('section', None, 'dp', 'mp')
- gain_grad: float32 [16, 4096], P('section', 'mp')
The draws below stay inside these ranges and needn't reach their ends.
Inputs may be any that keep to these rules, and one draw needn't show every extreme that they name: evicted is 0 for every section s >= 8; where it is 1, the stash lies in the spare_stash of section 15 - s.
All inputs are finite; a program needn't handle non-finite values.
Results may differ from the reference program's by a relative error of at most 0.023.
Values may be sent and summed in bfloat16 or wider, within the bound.
No kernel may reach another device: no remote copies, remote signals or barrier semaphores. Data moves between devices by JAX's collectives and lax.ppermute only.
A program may use at most 128 MiB of HBM per device.

```python
import jax
import jax.numpy as jnp
from jax import lax

MODEL_FEATURES = 4096
HEAD = 128
TOK = 128
TICKS = 3
SECTIONS = 16
TOKENS = 256
QCOL = 4096
KVCOL = 1024
N_DP = 2


def drawn_rows(key, shape):
    return jnp.clip(jax.random.normal(key, shape, jnp.float32), -6.0, 6.0)


def drawn_weights(key, shape):
    return jnp.clip(jax.random.normal(key, shape, jnp.float32), -6.0, 6.0) * MODEL_FEATURES ** (-0.5)


def draw_arriving(key, part):
    key = jax.random.fold_in(key, 31)
    shape = (SECTIONS, TOKENS, MODEL_FEATURES)
    return drawn_rows(key, shape).astype(jnp.bfloat16)


def draw_entering(key, part):
    key = jax.random.fold_in(key, 32)
    shape = (TICKS - 1, TOKENS, MODEL_FEATURES)
    return drawn_rows(key, shape).astype(jnp.bfloat16)


def draw_home_stash(key, part):
    key = jax.random.fold_in(key, 33)
    shape = (SECTIONS, TICKS, TOKENS, MODEL_FEATURES)
    return drawn_rows(key, shape).astype(jnp.bfloat16)


def draw_spare_stash(key, part):
    key = jax.random.fold_in(key, 34)
    shape = (SECTIONS, TICKS, TOKENS, MODEL_FEATURES)
    return drawn_rows(key, shape).astype(jnp.bfloat16)


def draw_query_weight_matrix(key, part):
    key = jax.random.fold_in(key, 21)
    base = drawn_weights(key, (SECTIONS, MODEL_FEATURES, QCOL))
    return base.astype(jnp.bfloat16)


def draw_key_weight_matrix(key, part):
    key = jax.random.fold_in(key, 22)
    base = drawn_weights(key, (SECTIONS, MODEL_FEATURES, KVCOL))
    return base.astype(jnp.bfloat16)


def draw_evicted(key, part):
    key = jax.random.fold_in(key, 11)
    coins = jax.random.randint(key, (SECTIONS, TICKS), 0, 2)
    early = (jnp.arange(SECTIONS) < SECTIONS // 2)[:, None]
    coins = coins.at[0, 0].set(1)
    return jnp.where(early, coins, 0).astype(jnp.int32)


def block_scale(stream_key, shape, pieces, smallest, top_value):
    loudness = 1.0
    for dim, parts in pieces:
        heights = jax.random.uniform(jax.random.fold_in(jax.random.fold_in(stream_key, 6), dim), (parts,), jnp.float32, smallest / len(pieces), top_value / len(pieces))
        loudness = loudness * jnp.repeat(jnp.exp(heights), shape[dim] // parts).reshape((-1,) + (1,) * (len(shape) - 1 - dim))
    return loudness


def normal_values(stream_key, dims, width, reach, shards=(), kind=jnp.bfloat16):
    values = width * jax.random.normal(stream_key, dims, jnp.float32)
    if shards:
        values = values * block_scale(stream_key, dims, shards, -0.22, 0.18)
    return jnp.clip(values, -reach, reach).astype(kind)


def setup_inputs(seed: int = 0) -> dict:
    arg_keys = jax.random.split(jax.random.key(seed), 13)
    return {
        "arriving": draw_arriving(jax.random.fold_in(arg_keys[12], 71), 0),
        "returning": normal_values(arg_keys[1], (SECTIONS, TOKENS, MODEL_FEATURES), 1.0, 6.0, ((0, 16), (1, 2), (2, 8))),
        "entering": draw_entering(jax.random.fold_in(arg_keys[12], 71), 0),
        "cot_entering": normal_values(arg_keys[3], (TICKS - 1, TOKENS, MODEL_FEATURES), 1.0, 6.0, ((1, 2), (2, 8))),
        "home_stash": draw_home_stash(jax.random.fold_in(arg_keys[12], 71), 0),
        "spare_stash": draw_spare_stash(jax.random.fold_in(arg_keys[12], 71), 0),
        "evicted": draw_evicted(jax.random.fold_in(arg_keys[12], 71), 0),
        "norm_gain": jnp.clip(1.0 + 0.15 * jax.random.normal(arg_keys[7], (SECTIONS, MODEL_FEATURES), jnp.float32), 0.25, 1.75),
        "query_weight_matrix": draw_query_weight_matrix(jax.random.fold_in(arg_keys[12], 71), 0),
        "key_weight_matrix": draw_key_weight_matrix(jax.random.fold_in(arg_keys[12], 71), 0),
        "value_weight_matrix": normal_values(arg_keys[10], (SECTIONS, MODEL_FEATURES, KVCOL), MODEL_FEATURES ** -0.5, 0.09375, ((0, 16), (2, 8))),
        "w_output": normal_values(arg_keys[11], (SECTIONS, QCOL, MODEL_FEATURES), QCOL ** -0.5, 0.09375, ((0, 16), (1, 8))),
    }


EPS = 1e-05

def attend(query_rows, key_row_block, value_row_block):
    length = query_rows.shape[0]
    groups = key_row_block.shape[1] // HEAD
    ratio = query_rows.shape[1] // key_row_block.shape[1]
    query_heads = query_rows.reshape(length, groups, ratio, HEAD)
    key_heads = key_row_block.reshape(length, groups, HEAD)
    value_heads = value_row_block.reshape(length, groups, HEAD)
    scores = jnp.einsum('tkgd,skd->kgts', query_heads, key_heads, precision=lax.Precision.HIGHEST) * HEAD ** (-0.5)
    causal = jnp.arange(length)[:, None] >= jnp.arange(length)[None, :]
    scores = jnp.where(causal, scores, jnp.float32(-1e+30))
    weights_soft = jax.nn.softmax(scores, axis=-1)
    mixed = jnp.einsum('kgts,skd->tkgd', weights_soft, value_heads, precision=lax.Precision.HIGHEST)
    return mixed.reshape(length, -1)

def batch_attend(query_rows, key_row_block, value_row_block):
    split = lambda arr: arr.reshape(N_DP, TOK, arr.shape[1])
    mixed = jax.vmap(attend)(split(query_rows), split(key_row_block), split(value_row_block))
    return mixed.reshape(N_DP * TOK, -1)

def apply_rms_norm(token_rows):
    floats = token_rows.astype(jnp.float32)
    root_mean_square = jnp.sqrt(lax.optimization_barrier(jnp.mean(floats * floats, axis=-1, keepdims=True)) + EPS)
    return (floats / root_mean_square, root_mean_square)

def apply_projection(token_rows, gain_as_row, query_weight_matrix, key_weight_matrix, value_weight_matrix):
    normalized_tokens, root_mean_square = apply_rms_norm(token_rows)
    normalized_input = (normalized_tokens * gain_as_row).astype(jnp.bfloat16)
    query_rows = jnp.dot(normalized_input, query_weight_matrix, preferred_element_type=jnp.float32).astype(jnp.bfloat16)
    key_row_block = jnp.dot(normalized_input, key_weight_matrix, preferred_element_type=jnp.float32).astype(jnp.bfloat16)
    value_row_block = jnp.dot(normalized_input, value_weight_matrix, preferred_element_type=jnp.float32).astype(jnp.bfloat16)
    return (normalized_tokens, root_mean_square, query_rows, key_row_block, value_row_block)

def contract_last(left, right):
    return lax.dot_general(left, right, (((1,), (1,)), ((), ())), preferred_element_type=jnp.float32)

def section_forward(token_rows, gain_as_row, query_weight_matrix, key_weight_matrix, value_weight_matrix, w_output):
    normalized_tokens, root_mean_square, query_rows, key_row_block, value_row_block = apply_projection(token_rows, gain_as_row, query_weight_matrix, key_weight_matrix, value_weight_matrix)
    attended = batch_attend(query_rows.astype(jnp.float32), key_row_block.astype(jnp.float32), value_row_block.astype(jnp.float32)).astype(jnp.bfloat16)
    outcome = jnp.dot(attended, w_output, preferred_element_type=jnp.float32)
    return (token_rows.astype(jnp.float32) + outcome).astype(jnp.bfloat16)

def section_backward(stored_inputs, incoming_cotangent, gain_as_row, query_weight_matrix, key_weight_matrix, value_weight_matrix, w_output):
    normalized_tokens, root_mean_square, query_rows, key_row_block, value_row_block = apply_projection(stored_inputs, gain_as_row, query_weight_matrix, key_weight_matrix, value_weight_matrix)
    d_att = contract_last(incoming_cotangent, w_output)
    unused, pullback = jax.vjp(batch_attend, query_rows.astype(jnp.float32), key_row_block.astype(jnp.float32), value_row_block.astype(jnp.float32))
    d_query, d_key, d_value = pullback(d_att)
    gradient_norm_input = contract_last(d_query.astype(jnp.bfloat16), query_weight_matrix)
    gradient_norm_input = gradient_norm_input + contract_last(d_key.astype(jnp.bfloat16), key_weight_matrix)
    gradient_norm_input = gradient_norm_input + contract_last(d_value.astype(jnp.bfloat16), value_weight_matrix)
    normalized_gradient = gradient_norm_input * gain_as_row
    square_statistic = lax.optimization_barrier(jnp.sum(normalized_gradient * normalized_tokens, axis=-1, keepdims=True))
    final_output = (incoming_cotangent.astype(jnp.float32) + (normalized_gradient - normalized_tokens * square_statistic / MODEL_FEATURES) / root_mean_square).astype(jnp.bfloat16)
    return (final_output, lax.optimization_barrier(jnp.sum(gradient_norm_input * normalized_tokens, axis=0)))

def reference(arriving, returning, entering, cot_entering, home_stash, spare_stash, evicted, norm_gain, query_weight_matrix, key_weight_matrix, value_weight_matrix, w_output):
    inputs_now = [arriving[index] for index in range(SECTIONS)]
    current_cotangents = [returning[index] for index in range(SECTIONS)]
    outputs_all = []
    cots_all = []
    gain_sums = [jnp.zeros((MODEL_FEATURES,), jnp.float32) for index in range(SECTIONS)]
    for tick_index in range(TICKS):
        outs_tick = []
        backs_tick = []
        for index in range(SECTIONS):
            params = (norm_gain[index], query_weight_matrix[index], key_weight_matrix[index], value_weight_matrix[index], w_output[index])
            outs_tick.append(section_forward(inputs_now[index], *params))
            stored_inputs = jnp.where(evicted[index, tick_index] == 1, spare_stash[SECTIONS - 1 - index, tick_index], home_stash[index, tick_index])
            back_rows, gain_part = section_backward(stored_inputs, current_cotangents[index], *params)
            backs_tick.append(back_rows)
            gain_sums[index] = gain_sums[index] + gain_part
        outputs_all.append(jnp.stack(outs_tick))
        cots_all.append(jnp.stack(backs_tick))
        if tick_index + 1 < TICKS:
            inputs_now = [entering[tick_index]] + outs_tick[:-1]
            current_cotangents = backs_tick[1:] + [cot_entering[tick_index]]
    section_outputs = jnp.stack(outputs_all, axis=1)
    section_cotangents = jnp.stack(cots_all, axis=1)
    return (section_outputs, section_cotangents, jnp.stack(gain_sums))
```

```python
import functools

import jax
import jax.numpy as jnp
from jax import lax
from jax.experimental import pallas as pl
from jax.experimental.pallas import tpu as pltpu
from jax.sharding import PartitionSpec as P

HEAD = 128
TICKS = 3
PARTS = 8
CHUNK = 512
ROWS = 128
KV = 128
HEADS = CHUNK // HEAD
QKV = CHUNK + 2 * KV
EPS = 1e-05
SCALE = HEAD**-0.5
F32 = jnp.float32
BF16 = jnp.bfloat16
NT = (((1,), (1,)), ((), ()))
TN = (((0,), (0,)), ((), ()))
VMEM = pl.BlockSpec(memory_space=pltpu.VMEM)
SMEM = pl.BlockSpec(memory_space=pltpu.SMEM)


def call(kernel, outs, ins, me, flops, bytes_accessed, vmem=48):
    return pl.pallas_call(
        kernel,
        out_shape=outs,
        in_specs=[SMEM] + [VMEM] * len(ins),
        out_specs=[VMEM] * len(outs),
        compiler_params=pltpu.CompilerParams(vmem_limit_bytes=vmem * 2**20),
        cost_estimate=pl.CostEstimate(
            flops=flops, bytes_accessed=bytes_accessed, transcendentals=0
        ),
    )(me, *ins)


def dot(a, b, dims=(((1,), (0,)), ((), ()))):
    return lax.dot_general(a, b, dims, preferred_element_type=F32)


def project(chunks, starts, gain, wq, wk, wv):
    rows = chunks[0].shape[0]
    squares = jnp.zeros((rows, 1), F32)
    q = jnp.zeros((rows, CHUNK), F32)
    k = jnp.zeros((rows, KV), F32)
    v = jnp.zeros((rows, KV), F32)
    for chunk, start in zip(chunks, starts):
        x = chunk.astype(F32)
        squares += jnp.sum(x * x, axis=1, keepdims=True)
        xg = (x * gain[:, pl.ds(start, CHUNK)]).astype(BF16)
        q += dot(xg, wq[pl.ds(start, CHUNK), :])
        k += dot(xg, wk[pl.ds(start, CHUNK), :])
        v += dot(xg, wv[pl.ds(start, CHUNK), :])
    root = jnp.sqrt(squares / (PARTS * CHUNK) + EPS)
    inverse = 1.0 / root
    return (q * inverse).astype(BF16), (k * inverse).astype(BF16), (v * inverse).astype(BF16), root


def start_of(me, k):
    return pl.multiple_of((me ^ k) * CHUNK, CHUNK)


def heads_down(wide):
    return jnp.concatenate([wide[:, h * HEAD : (h + 1) * HEAD] for h in range(HEADS)], axis=0)


def heads_across(tall):
    return jnp.concatenate([tall[h * ROWS : (h + 1) * ROWS] for h in range(HEADS)], axis=1)


def causal_scores(q, k):
    scores = dot(q, k, NT) * SCALE
    row = lax.broadcasted_iota(jnp.int32, scores.shape, 0) & (ROWS - 1)
    column = lax.broadcasted_iota(jnp.int32, scores.shape, 1)
    return jnp.where(row >= column, scores, F32(-1e30))


def forward_kernel(me_ref, *refs):
    chunks, (gain, wq, wk, wv, attended) = refs[:PARTS], refs[PARTS:]
    me = me_ref[0]
    q, k, v, _ = project(
        [c[...] for c in chunks], [start_of(me, i) for i in range(PARTS)], gain, wq, wk, wv
    )
    scores = causal_scores(heads_down(q), k)
    weights = jnp.exp(scores - jnp.max(scores, axis=1, keepdims=True))
    total = jnp.sum(weights, axis=1, keepdims=True)
    mixed = dot(weights.astype(BF16), v) / total
    attended[...] = heads_across(mixed).astype(BF16)


def out_kernel(me_ref, attended, wo, p2, p1, p3, mine):
    me = me_ref[0]
    a = attended[...]
    for ref, j in ((p2, 2), (p1, 1), (p3, 3), (mine, 0)):
        for half in range(2):
            part = dot(a, wo[:, pl.ds(start_of(me, j ^ (4 * half)), CHUNK)])
            ref[:, half * CHUNK : (half + 1) * CHUNK] = part.astype(ref.dtype)


def recompute_near_kernel(me_ref, *refs):
    chunks, (gain, wq, wk, wv, qkv, root) = refs[:PARTS], refs[PARTS:]
    me = me_ref[0]
    q, k, v, r = project(
        [c[...] for c in chunks], [start_of(me, i) for i in range(PARTS)], gain, wq, wk, wv
    )
    qkv[:, :CHUNK] = q
    qkv[:, CHUNK : CHUNK + KV] = k
    qkv[:, CHUNK + KV :] = v
    root[...] = jnp.broadcast_to(r, root.shape)


def recompute_far_kernel(me_ref, stash, gain, wq, wk, wv, qkv, root):
    q, k, v, r = project(
        [stash[i] for i in range(PARTS)], [i * CHUNK for i in range(PARTS)], gain, wq, wk, wv
    )
    qkv[:, :CHUNK] = q
    qkv[:, CHUNK : CHUNK + KV] = k
    qkv[:, CHUNK + KV :] = v
    root[...] = jnp.broadcast_to(r, root.shape)


def backward_kernel(me_ref, *refs):
    chunks, (qkv, wo, d_qkv, stat) = refs[:PARTS], refs[PARTS:]
    me = me_ref[0]
    d_att = jnp.zeros((ROWS, CHUNK), F32)
    for i, chunk in enumerate(chunks):
        d_att += dot(chunk[...], wo[:, pl.ds(start_of(me, i), CHUNK)], NT)
    q = heads_down(qkv[:, :CHUNK])
    k = qkv[:, CHUNK : CHUNK + KV]
    v = qkv[:, CHUNK + KV :]
    d_out = heads_down(d_att).astype(BF16)
    scores = causal_scores(q, k)
    weights = jnp.exp(scores - jnp.max(scores, axis=1, keepdims=True))
    weights = weights / jnp.sum(weights, axis=1, keepdims=True)
    d_weights = dot(d_out, v, NT)
    centre = jnp.sum(d_weights * weights, axis=1, keepdims=True)
    d_scores = (weights * (d_weights - centre) * SCALE).astype(BF16)
    d_q = heads_across(dot(d_scores, k)).astype(BF16)
    d_k = dot(d_scores, q, TN).astype(BF16)
    d_v = dot(weights.astype(BF16), d_out, TN).astype(BF16)
    d_qkv[:, :CHUNK] = d_q
    d_qkv[:, CHUNK : CHUNK + KV] = d_k
    d_qkv[:, CHUNK + KV :] = d_v
    product = d_qkv[...].astype(F32) * qkv[...].astype(F32)
    stat[...] = jnp.broadcast_to(jnp.sum(product, axis=1, keepdims=True), stat.shape)


def norm_cotangent_kernel(me_ref, d_qkv, stat, wq, wk, wv, p2, p1, p3, mine):
    me = me_ref[0]
    d_q, d_k, d_v = d_qkv[:, :CHUNK], d_qkv[:, CHUNK : CHUNK + KV], d_qkv[:, CHUNK + KV :]
    s = stat[...]
    high = s.astype(BF16)
    low = (s - high.astype(F32)).astype(BF16)
    lane = lax.broadcasted_iota(jnp.int32, s.shape, 1)
    packed = jnp.where(lane == 0, high.astype(F32), low.astype(F32)).astype(BF16)
    for ref, j in ((p2, 2), (p1, 1), (p3, 3), (mine, 0)):
        for half in range(2):
            start = start_of(me, j ^ (4 * half))
            rows = pl.ds(start, CHUNK)
            part = dot(d_q, wq[rows, :], NT) + dot(d_k, wk[rows, :], NT) + dot(d_v, wv[rows, :], NT)
            ref[:, half * CHUNK : (half + 1) * CHUNK] = part.astype(ref.dtype)
        if j:
            ref[:, 2 * CHUNK :] = packed


def swap(value, mask):
    return lax.ppermute(value, "mp", [(i, i ^ mask) for i in range(PARTS)])


def gather(mine):
    other = swap(mine, 4)
    near = {j: swap(mine, j) for j in (2, 1, 3)}
    far = {j: swap(other, j) for j in (2, 1, 3)}
    return [mine, near[1], near[2], near[3], other, far[1], far[2], far[3]]


def unpack_stat(packed):
    wide = packed.astype(F32)
    return wide[:, 0:1] + wide[:, 1:2]


def pack_stat(s):
    high = s.astype(BF16)
    low = (s - high.astype(F32)).astype(BF16)
    return jnp.concatenate([high, jnp.broadcast_to(low, (s.shape[0], KV - 1))], axis=1)


def on_device(
    arriving,
    returning,
    entering,
    cot_entering,
    home_stash,
    spare_stash,
    evicted,
    norm_gain,
    query_weight_matrix,
    key_weight_matrix,
    value_weight_matrix,
    w_output,
):
    sections = lax.axis_size("section")
    section = lax.axis_index("section")
    place = lax.axis_index("mp")
    me = place.astype(jnp.int32).reshape(1)
    gain = norm_gain
    gain_mine = lax.dynamic_slice_in_dim(norm_gain, place * CHUNK, CHUNK, 1)
    wq, wk, wv, wo = (
        query_weight_matrix[0],
        key_weight_matrix[0],
        value_weight_matrix[0],
        w_output[0],
    )
    mirror = [(sections - 1 - s, s) for s in range(sections // 2)]
    up = [(s, (s + 1) % sections) for s in range(sections)]
    down = [((s + 1) % sections, s) for s in range(sections)]

    fetched_first = lax.ppermute(spare_stash[0, 0], "section", mirror)
    fetched_rest = lax.ppermute(spare_stash[0, 1:], "section", mirror)
    stash_first = jnp.where(evicted[0, 0] == 1, fetched_first, home_stash[0, 0])
    stash_rest = jnp.where(
        evicted[0, 1:, None, None] == 1, fetched_rest, home_stash[0, 1:]
    ).reshape((TICKS - 1) * ROWS, CHUNK)
    full_rest = lax.all_gather(stash_rest, "mp")
    wide = lambda rows, columns, kind: jax.ShapeDtypeStruct((rows, columns), kind)

    inputs_now = arriving[0]
    cots_now = returning[0]
    saved = []
    outputs, cots = [], []
    gain_total = jnp.zeros((1, CHUNK), F32)
    for tick in range(TICKS):
        x_all = gather(inputs_now)
        attended = call(
            forward_kernel,
            [wide(ROWS, CHUNK, BF16)],
            x_all + [gain, wq, wk, wv],
            me,
            2 * ROWS * 4096 * QKV,
            7 * 2**20,
        )[0]
        if tick == 0:
            qkv, root = call(
                recompute_near_kernel,
                [wide(ROWS, QKV, BF16), wide(ROWS, KV, F32)],
                gather(stash_first) + [gain, wq, wk, wv],
                me,
                2 * ROWS * 4096 * QKV,
                7 * 2**20,
            )
            saved.append((qkv, root, stash_first))
        if tick == 1:
            rows = (TICKS - 1) * ROWS
            qkv, root = call(
                recompute_far_kernel,
                [wide(rows, QKV, BF16), wide(rows, KV, F32)],
                [full_rest, gain, wq, wk, wv],
                me,
                2 * rows * 4096 * QKV,
                8 * 2**20,
            )
            for t in range(TICKS - 1):
                part = slice(t * ROWS, (t + 1) * ROWS)
                saved.append((qkv[part], root[part], stash_rest[part]))
        c_all = gather(cots_now)
        p2, p1, p3, mine = call(
            out_kernel,
            [wide(ROWS, 2 * CHUNK, BF16)] * 3 + [wide(ROWS, 2 * CHUNK, F32)],
            [attended, wo],
            me,
            2 * ROWS * 4096 * CHUNK,
            5 * 2**20,
        )
        sent = [swap(p2, 2), swap(p1, 1), swap(p3, 3)]
        total = mine
        for piece in sent:
            total = total + piece.astype(F32)
        crossed = swap(total[:, CHUNK:].astype(BF16), 4)
        result = (inputs_now.astype(F32) + total[:, :CHUNK] + crossed.astype(F32)).astype(BF16)
        outputs.append(result)
        if tick + 1 < TICKS:
            next_inputs = lax.ppermute(
                jnp.where(section == sections - 1, entering[tick], result), "section", up
            )

        qkv, root, stashed = saved[tick]
        d_qkv, stat = call(
            backward_kernel,
            [wide(ROWS, QKV, BF16), wide(ROWS, KV, F32)],
            c_all + [qkv, wo],
            me,
            2 * ROWS * 4096 * CHUNK,
            6 * 2**20,
        )
        b2, b1, b3, b_mine = call(
            norm_cotangent_kernel,
            [wide(ROWS, 2 * CHUNK + KV, BF16)] * 3 + [wide(ROWS, 2 * CHUNK, F32)],
            [d_qkv, stat, wq, wk, wv],
            me,
            2 * ROWS * 4096 * QKV,
            7 * 2**20,
        )
        sent = [swap(b2, 2), swap(b1, 1), swap(b3, 3)]
        total = b_mine
        stat_total = stat[:, :1]
        for piece in sent:
            total = total + piece[:, : 2 * CHUNK].astype(F32)
            stat_total = stat_total + unpack_stat(piece[:, 2 * CHUNK :])
        crossed = swap(
            jnp.concatenate([total[:, CHUNK:].astype(BF16), pack_stat(stat_total)], axis=1), 4
        )
        d_norm = total[:, :CHUNK] + crossed[:, :CHUNK].astype(F32)
        mean = (stat_total + unpack_stat(crossed[:, CHUNK:])) / (PARTS * CHUNK)
        r = root[:, :1]
        xhat = stashed.astype(F32) / r
        back = (cots_now.astype(F32) + (d_norm * gain_mine - xhat * mean) / r).astype(BF16)
        gain_total = gain_total + jnp.sum(d_norm * xhat, axis=0, keepdims=True)
        cots.append(back)
        if tick + 1 < TICKS:
            cots_now = lax.ppermute(
                jnp.where(section == 0, cot_entering[tick], back), "section", down
            )
            inputs_now = next_inputs
    gain_grad = gain_total + lax.ppermute(gain_total, "dp", [(0, 1), (1, 0)])
    return (jnp.stack(outputs)[None], jnp.stack(cots)[None], gain_grad)


def solution(mesh):
    placed = (
        P("section", "dp", "mp"),
        P("section", "dp", "mp"),
        P(None, "dp", "mp"),
        P(None, "dp", "mp"),
        P("section", None, "dp", "mp"),
        P("section", None, "dp", "mp"),
        P("section", None),
        P("section", None),
        P("section", None, "mp"),
        P("section", None, "mp"),
        P("section", None, "mp"),
        P("section", "mp", None),
    )
    return jax.shard_map(
        on_device,
        mesh=mesh,
        in_specs=placed,
        out_specs=(
            P("section", None, "dp", "mp"),
            P("section", None, "dp", "mp"),
            P("section", "mp"),
        ),
        check_vma=False,
    )
```

```python
import functools

import jax
import jax.numpy as jnp
from jax import lax
from jax.experimental import pallas as pl
from jax.experimental.pallas import tpu as pltpu
from jax.sharding import PartitionSpec as P

HEAD = 128
TICKS = 3
PARTS = 8
CHUNK = 512
ROWS = 128
KV = 128
HEADS = CHUNK // HEAD
QKV = CHUNK + 2 * KV
EPS = 1e-05
SCALE = HEAD**-0.5
F32 = jnp.float32
BF16 = jnp.bfloat16
NT = (((1,), (1,)), ((), ()))
TN = (((0,), (0,)), ((), ()))
VMEM_LIMIT = 48 * 2**20
VMEM = pl.BlockSpec(memory_space=pltpu.VMEM)
ANY = pl.BlockSpec(memory_space=pl.ANY)
SMEM = pl.BlockSpec(memory_space=pltpu.SMEM)


def call(kernel, outs, ins, me, after=(), weights=()):
    count = len(ins) + len(weights)

    name = getattr(kernel, "func", kernel).__name__

    def body(place_ref, *refs):
        kernel(place_ref, *refs[:count], *refs[count + len(after) :])

    return pl.pallas_call(
        body,
        out_shape=outs,
        in_specs=[SMEM] + [VMEM] * count + [ANY] * len(after),
        out_specs=[VMEM] * len(outs),
        compiler_params=pltpu.CompilerParams(vmem_limit_bytes=VMEM_LIMIT),
        cost_estimate=pl.CostEstimate(flops=1, bytes_accessed=1, transcendentals=0),
        name=name,
    )(me, *ins, *weights, *after)


def dot(a, b, dims=(((1,), (0,)), ((), ()))):
    return lax.dot_general(a, b, dims, preferred_element_type=F32)


def project(chunks, starts, gain, wq, wk, wv):
    rows = chunks[0].shape[0]
    squares = jnp.zeros((rows, 1), F32)
    q = jnp.zeros((rows, CHUNK), F32)
    k = jnp.zeros((rows, KV), F32)
    v = jnp.zeros((rows, KV), F32)
    for chunk, start in zip(chunks, starts):
        x = chunk.astype(F32)
        squares += jnp.sum(x * x, axis=1, keepdims=True)
        xg = (x * gain[:, pl.ds(start, CHUNK)]).astype(BF16)
        q += dot(xg, wq[pl.ds(start, CHUNK), :])
        k += dot(xg, wk[pl.ds(start, CHUNK), :])
        v += dot(xg, wv[pl.ds(start, CHUNK), :])
    root = jnp.sqrt(squares / (PARTS * CHUNK) + EPS)
    inverse = 1.0 / root
    return (q * inverse).astype(BF16), (k * inverse).astype(BF16), (v * inverse).astype(BF16), root


def start_of(me, k):
    return pl.multiple_of((me ^ k) * CHUNK, CHUNK)


def heads_down(wide):
    return jnp.concatenate([wide[:, h * HEAD : (h + 1) * HEAD] for h in range(HEADS)], axis=0)


def heads_across(tall):
    return jnp.concatenate([tall[h * ROWS : (h + 1) * ROWS] for h in range(HEADS)], axis=1)


def causal_scores(q, k):
    scores = dot(q, k, NT) * SCALE
    row = lax.broadcasted_iota(jnp.int32, scores.shape, 0) & (ROWS - 1)
    column = lax.broadcasted_iota(jnp.int32, scores.shape, 1)
    return jnp.where(row >= column, scores, F32(-1e30))


FORWARD, BACKWARD, STASH = (4, 1, 3), (3, 4, 1), (1, 3, 4)
SPREAD = (0, 4, 2, 6, 1, 5, 3, 7)


def hypercube_masks(order):
    masks = (0,)
    for step in order:
        masks += tuple(m ^ step for m in masks)
    return masks


def chunks_of(pieces):
    return [p[:, i : i + CHUNK] for p in pieces for i in range(0, p.shape[1], CHUNK)]


def starts_of(me, masks):
    return [start_of(me, m) for m in masks]


def forward_kernel(masks, place_ref, *refs):
    pieces, (gain, wq, wk, wv, attended) = refs[:-5], refs[-5:]
    starts = starts_of(place_ref[0], masks)
    q, k, v, _ = project(chunks_of(pieces), starts, gain, wq, wk, wv)
    scores = causal_scores(heads_down(q), k)
    weights = jnp.exp(scores - jnp.max(scores, axis=1, keepdims=True))
    total = jnp.sum(weights, axis=1, keepdims=True)
    mixed = dot(weights.astype(BF16), v) / total
    attended[...] = heads_across(mixed).astype(BF16)


def scatter_starts(me):
    return [start_of(me, j ^ half) for j in (2, 1, 3, 0) for half in (0, 4)]


def put_part(refs, i, part):
    ref, column = refs[i // 2], (i % 2) * CHUNK
    ref[:, column : column + CHUNK] = part.astype(ref.dtype)


def out_kernel(place_ref, attended, wo, p2, p1, p3, mine):
    for i, start in enumerate(scatter_starts(place_ref[0])):
        put_part((p2, p1, p3, mine), i, dot(attended[...], wo[:, pl.ds(start, CHUNK)]))


def forward_sum_kernel(tick, place_ref, mine, p2, p1, p3, x, edge, relayed, crossing, total):
    t = mine[...] + p2[...].astype(F32) + p1[...].astype(F32) + p3[...].astype(F32)
    own, other = t[:, :CHUNK], t[:, CHUNK:]
    own = own + x[:, :CHUNK].astype(F32)
    total[...] = own
    crossing[...] = other.astype(BF16)
    last = place_ref[2] == 1
    relayed[:, :CHUNK] = jnp.where(last, edge[tick].astype(F32), own).astype(BF16)
    relayed[:, CHUNK:] = jnp.where(last, 0.0, other).astype(BF16)


def keep(q, k, v, r, own, other, qkv, xhat, root):
    qkv[:, :CHUNK] = q
    qkv[:, CHUNK : CHUNK + KV] = k
    qkv[:, CHUNK + KV :] = v
    root[...] = jnp.broadcast_to(r, root.shape)
    xhat[:, :CHUNK] = own.astype(F32) / r
    xhat[:, CHUNK:] = other.astype(F32) / r


def recompute_near_kernel(masks, place_ref, *refs):
    pieces, (gain, wq, wk, wv, qkv, xhat, root) = refs[:-7], refs[-7:]
    chunks = chunks_of(pieces)
    starts = starts_of(place_ref[0], masks)
    q, k, v, r = project(chunks, starts, gain, wq, wk, wv)
    keep(q, k, v, r, chunks[masks.index(0)], chunks[masks.index(4)], qkv, xhat, root)


def recompute_far_kernel(place_ref, stash, gain, wq, wk, wv, qkv, xhat, root):
    me = place_ref[0]
    q, k, v, r = project(
        [stash[i] for i in range(PARTS)],
        [i * CHUNK for i in range(PARTS)],
        gain,
        wq,
        wk,
        wv,
    )
    keep(q, k, v, r, stash[me], stash[me ^ 4], qkv, xhat, root)


def backward_kernel(masks, row, place_ref, *refs):
    pieces, (qkv, wo, d_qkv, stat) = refs[:-4], refs[-4:]
    qkv = qkv.at[row : row + ROWS]
    d_att = jnp.zeros((ROWS, CHUNK), F32)
    for chunk, start in zip(chunks_of(pieces), starts_of(place_ref[0], masks)):
        d_att += dot(chunk, wo[:, pl.ds(start, CHUNK)], NT)
    q = heads_down(qkv[:, :CHUNK])
    k = qkv[:, CHUNK : CHUNK + KV]
    v = qkv[:, CHUNK + KV :]
    d_out = heads_down(d_att).astype(BF16)
    scores = causal_scores(q, k)
    weights = jnp.exp(scores - jnp.max(scores, axis=1, keepdims=True))
    weights = weights / jnp.sum(weights, axis=1, keepdims=True)
    d_weights = dot(d_out, v, NT)
    centre = jnp.sum(d_weights * weights, axis=1, keepdims=True)
    d_scores = (weights * (d_weights - centre) * SCALE).astype(BF16)
    d_q = heads_across(dot(d_scores, k)).astype(BF16)
    d_k = dot(d_scores, q, TN).astype(BF16)
    d_v = dot(weights.astype(BF16), d_out, TN).astype(BF16)
    d_qkv[:, :CHUNK] = d_q
    d_qkv[:, CHUNK : CHUNK + KV] = d_k
    d_qkv[:, CHUNK + KV :] = d_v
    product = d_qkv[...].astype(F32) * qkv[...].astype(F32)
    stat[...] = jnp.broadcast_to(jnp.sum(product, axis=1, keepdims=True), stat.shape)


def pack_stat(s):
    high = s.astype(BF16).astype(F32)
    lane = lax.broadcasted_iota(jnp.int32, (ROWS, KV), 1)
    return jnp.where(lane == 0, high, s - high).astype(BF16)


def unpack_stat(packed):
    wide = packed.astype(F32)
    return wide[:, 0:1] + wide[:, 1:2]


def norm_cotangent_kernel(place_ref, d_qkv, stat, wq, wk, wv, p2, p1, p3, mine):
    packed = pack_stat(stat[:, :1])
    for p in (p2, p1, p3):
        p[:, 2 * CHUNK :] = packed
    d_q, d_k, d_v = d_qkv[:, :CHUNK], d_qkv[:, CHUNK : CHUNK + KV], d_qkv[:, CHUNK + KV :]
    for i, start in enumerate(scatter_starts(place_ref[0])):
        rows = pl.ds(start, CHUNK)
        part = dot(d_q, wq[rows, :], NT) + dot(d_k, wk[rows, :], NT) + dot(d_v, wv[rows, :], NT)
        put_part((p2, p1, p3, mine), i, part)


def backward_sum_kernel(
    tick, row, place_ref, mine, stat, p2, p1, p3, xhat, root, gain, c, edge, relayed, crossing, total, stat_out
):
    me = place_ref[0]
    t = mine[...]
    s = stat[:, :1]
    for p in (p2, p1, p3):
        t = t + p[:, : 2 * CHUNK].astype(F32)
        s = s + unpack_stat(p[:, 2 * CHUNK :])
    own, other = t[:, :CHUNK], t[:, CHUNK:]
    total[...] = own
    stat_out[...] = jnp.broadcast_to(s, stat_out.shape)
    crossing[:, :CHUNK] = other.astype(BF16)
    crossing[:, CHUNK:] = pack_stat(s)
    mean = s / (PARTS * CHUNK)
    rows = slice(row, row + ROWS)
    xhat = xhat[rows, :]
    inverse = 1.0 / root[rows, :1]
    near = (own * gain[:, pl.ds(start_of(me, 0), CHUNK)] - xhat[:, :CHUNK] * mean) * inverse
    far = (other * gain[:, pl.ds(start_of(me, 4), CHUNK)] - xhat[:, CHUNK:] * mean) * inverse
    near = near + c[:, :CHUNK].astype(F32)
    first = place_ref[1] == 1
    relayed[:, :CHUNK] = jnp.where(first, edge[tick].astype(F32), near).astype(BF16)
    relayed[:, CHUNK:] = jnp.where(first, 0.0, far).astype(BF16)


def merge_kernel(place_ref, straight, across, pair):
    for half in (0, CHUNK):
        other = across[:, CHUNK - half : 2 * CHUNK - half].astype(F32)
        total = straight[:, half : half + CHUNK].astype(F32) + other
        pair[:, half : half + CHUNK] = total.astype(BF16)


def swap(value, mask):
    return lax.ppermute(value, "mp", [(i, i ^ mask) for i in range(PARTS)])


def spread(pair):
    far = {j: swap(pair, j) for j in (2, 1, 3)}
    return [pair, far[2], far[1], far[3]]


def gather(mine, order):
    for step in order[:-1]:
        mine = jnp.concatenate([mine, swap(mine, step)], axis=1)
    return [mine, swap(mine, order[-1])]


def relay(payload, step, sections, me, after=()):
    def pairs(mask):
        return [
            (s * PARTS + i, (s + step) % sections * PARTS + (i ^ mask))
            for s in range(sections)
            for i in range(PARTS)
        ]

    straight = lax.ppermute(payload, ("section", "mp"), pairs(0))
    across = lax.ppermute(payload, ("section", "mp"), pairs(4))
    shape = jax.ShapeDtypeStruct((ROWS, 2 * CHUNK), BF16)
    return call(merge_kernel, [shape], [straight, across], me, after)[0]


def on_device(
    arriving,
    returning,
    entering,
    cot_entering,
    home_stash,
    spare_stash,
    evicted,
    norm_gain,
    query_weight_matrix,
    key_weight_matrix,
    value_weight_matrix,
    w_output,
):
    sections = lax.axis_size("section")
    section = lax.axis_index("section")
    place = lax.axis_index("mp")
    me = jnp.stack([place, section == 0, section == sections - 1]).astype(jnp.int32)
    gain = norm_gain
    gain_mine = lax.dynamic_slice_in_dim(norm_gain, place * CHUNK, CHUNK, 1)
    wq, wk, wv, wo = (
        query_weight_matrix[0],
        key_weight_matrix[0],
        value_weight_matrix[0],
        w_output[0],
    )
    mirror = [(sections - 1 - s, s) for s in range(sections // 2)]
    wide = lambda rows, columns, kind: jax.ShapeDtypeStruct((rows, columns), kind)
    rest = (TICKS - 1) * ROWS

    x_all = gather(arriving[0], FORWARD)
    c_all = gather(returning[0], BACKWARD)
    fetched_first = lax.ppermute(spare_stash[0, 0], "section", mirror)
    home_first = jnp.where(evicted[0, 0] == 2, x_all[0][:, 2 * CHUNK : 3 * CHUNK], home_stash[0, 0])
    stash_first = jnp.where(evicted[0, 0] == 1, fetched_first, home_first)
    spare_rest = jnp.where(evicted[0, 0] == 2, fetched_first, spare_stash[0, 1:])
    fetched_rest = lax.ppermute(spare_rest, "section", mirror)
    saved = []
    forward_totals, backward_totals, crossings = [], [], []
    before = []
    for tick in range(TICKS):
        final = tick + 1 == TICKS
        edge = min(tick, TICKS - 2)
        row = max(tick - 1, 0) * ROWS
        attended = call(
            functools.partial(forward_kernel, hypercube_masks(FORWARD) if tick == 0 else SPREAD),
            [wide(ROWS, CHUNK, BF16)],
            x_all + [gain],
            me,
            before,
            [wq, wk, wv],
        )[0]
        p2, p1, p3, mine = call(
            out_kernel,
            [wide(ROWS, 2 * CHUNK, BF16)] * 3 + [wide(ROWS, 2 * CHUNK, F32)],
            [attended],
            me,
            (),
            [wo],
        )
        f_parts = [mine, swap(p2, 2), swap(p1, 1), swap(p3, 3)]
        if tick == 0:
            kept = call(
                functools.partial(recompute_near_kernel, hypercube_masks(STASH)),
                [wide(ROWS, QKV, BF16), wide(ROWS, 2 * CHUNK, F32), wide(ROWS, KV, F32)],
                gather(stash_first, STASH) + [gain],
                me,
                [mine] + c_all[1:],
                [wq, wk, wv],
                )
            saved.append(kept)
        if tick == 1:
            far = call(
                recompute_far_kernel,
                [wide(rest, QKV, BF16), wide(rest, 2 * CHUNK, F32), wide(rest, KV, F32)],
                [full_rest, gain],
                me,
                [mine],
                [wq, wk, wv],
                )
            saved += [far] * (TICKS - 1)
        qkv, xhat, root = saved[tick]
        d_qkv, stat = call(
            functools.partial(
                backward_kernel, hypercube_masks(BACKWARD) if tick == 0 else SPREAD, row
            ),
            [wide(ROWS, QKV, BF16), wide(ROWS, KV, F32)],
            c_all + [qkv],
            me,
            [mine],
            [wo],
        )
        b2, b1, b3, b_mine = call(
            norm_cotangent_kernel,
            [wide(ROWS, 2 * CHUNK + KV, BF16)] * 3 + [wide(ROWS, 2 * CHUNK, F32)],
            [d_qkv, stat],
            me,
            (),
            [wq, wk, wv],
        )
        b_parts = [b_mine, stat, swap(b2, 2), swap(b1, 1), swap(b3, 3)]
        relayed, crossing, total = call(
            functools.partial(forward_sum_kernel, edge),
            [wide(ROWS, 2 * CHUNK, BF16), wide(ROWS, CHUNK, BF16), wide(ROWS, CHUNK, F32)],
            f_parts + [x_all[0], entering],
            me,
            [b_mine],
        )
        if tick == 0:
            home_rest = jnp.where(evicted[0, 0] == 2, crossing, home_stash[0, 1:])
            stash_rest = jnp.where(evicted[0, 1:, None, None] == 1, fetched_rest, home_rest)
            full_rest = lax.all_gather(stash_rest.reshape(rest, CHUNK), "mp")
        before = [crossing]
        if not final:
            x_all = spread(relay(relayed, 1, sections, me))
            before = [x_all[0]]
        forward_totals.append(total)
        crossings.append(crossing)

        c = c_all[0]
        relayed, crossing, total, stat = call(
            functools.partial(backward_sum_kernel, edge, row),
            [
                wide(ROWS, 2 * CHUNK, BF16),
                wide(ROWS, CHUNK + KV, BF16),
                wide(ROWS, CHUNK, F32),
                wide(ROWS, KV, F32),
            ],
            b_parts + [xhat, root, gain, c, cot_entering],
            me,
            before,
        )
        if not final:
            c_all = spread(relay(relayed, -1, sections, me, x_all[1:]))
            before = [c_all[0]]
        rows = slice(row, row + ROWS)
        backward_totals.append((total, stat, xhat[rows, :CHUNK], root[rows, :1], c[:, :CHUNK]))
        crossings.append(crossing)

    early = swap(jnp.concatenate(crossings[:-2], axis=1), 4)
    crossed = []
    for crossing in crossings[:-2]:
        crossed.append(early[:, : crossing.shape[1]])
        early = early[:, crossing.shape[1] :]
    crossed += [swap(crossing, 4) for crossing in crossings[-2:]]
    outputs, cots = [], []
    gain_total = jnp.zeros((1, CHUNK), F32)
    for tick in range(TICKS):
        forward, backward = crossed[2 * tick : 2 * tick + 2]
        outputs.append((forward_totals[tick] + forward.astype(F32)).astype(BF16))
        total, stat, xhat, root, c = backward_totals[tick]
        d_norm = total + backward[:, :CHUNK].astype(F32)
        mean = (stat[:, :1] + unpack_stat(backward[:, CHUNK:])) / (PARTS * CHUNK)
        back = c.astype(F32) + (d_norm * gain_mine - xhat * mean) / root
        cots.append(back.astype(BF16))
        gain_total = gain_total + jnp.sum(d_norm * xhat, axis=0, keepdims=True)
    gain_grad = gain_total + lax.ppermute(gain_total, "dp", [(0, 1), (1, 0)])
    return (jnp.stack(outputs)[None], jnp.stack(cots)[None], gain_grad)


def solution(mesh):
    placed = (
        P("section", "dp", "mp"),
        P("section", "dp", "mp"),
        P(None, "dp", "mp"),
        P(None, "dp", "mp"),
        P("section", None, "dp", "mp"),
        P("section", None, "dp", "mp"),
        P("section", None),
        P("section", None),
        P("section", None, "mp"),
        P("section", None, "mp"),
        P("section", None, "mp"),
        P("section", "mp", None),
    )
    return jax.shard_map(
        on_device,
        mesh=mesh,
        in_specs=placed,
        out_specs=(
            P("section", None, "dp", "mp"),
            P("section", None, "dp", "mp"),
            P("section", "mp"),
        ),
        check_vma=False,
    )
```

```python
import functools

import jax
import jax.numpy as jnp
from jax import lax
from jax.experimental import pallas as pl
from jax.experimental.pallas import tpu as pltpu
from jax.sharding import PartitionSpec as P

HEAD = 128
TICKS = 3
PARTS = 8
CHUNK = 512
ROWS = 128
KV = 128
HEADS = CHUNK // HEAD
QKV = CHUNK + 2 * KV
EPS = 1e-05
SCALE = HEAD**-0.5
F32 = jnp.float32
BF16 = jnp.bfloat16
NT = (((1,), (1,)), ((), ()))
TN = (((0,), (0,)), ((), ()))
VMEM_LIMIT = 48 * 2**20
VMEM = pl.BlockSpec(memory_space=pltpu.VMEM)
ANY = pl.BlockSpec(memory_space=pl.ANY)
SMEM = pl.BlockSpec(memory_space=pltpu.SMEM)


def call(kernel, outs, ins, me, after=(), weights=()):
    count = len(ins) + len(weights)

    name = getattr(kernel, "func", kernel).__name__

    def body(place_ref, *refs):
        kernel(place_ref, *refs[:count], *refs[count + len(after) :])

    return pl.pallas_call(
        body,
        out_shape=outs,
        in_specs=[SMEM] + [VMEM] * count + [ANY] * len(after),
        out_specs=[VMEM] * len(outs),
        compiler_params=pltpu.CompilerParams(vmem_limit_bytes=VMEM_LIMIT),
        cost_estimate=pl.CostEstimate(flops=1, bytes_accessed=1, transcendentals=0),
        name=name,
    )(me, *ins, *weights, *after)


def dot(a, b, dims=(((1,), (0,)), ((), ()))):
    return lax.dot_general(a, b, dims, preferred_element_type=F32)


def project(chunks, starts, gain, wq, wk, wv):
    rows = chunks[0].shape[0]
    squares = jnp.zeros((rows, 1), F32)
    q = jnp.zeros((rows, CHUNK), F32)
    k = jnp.zeros((rows, KV), F32)
    v = jnp.zeros((rows, KV), F32)
    for chunk, start in zip(chunks, starts):
        x = chunk.astype(F32)
        squares += jnp.sum(x * x, axis=1, keepdims=True)
        xg = (x * gain[:, pl.ds(start, CHUNK)]).astype(BF16)
        q += dot(xg, wq[pl.ds(start, CHUNK), :])
        k += dot(xg, wk[pl.ds(start, CHUNK), :])
        v += dot(xg, wv[pl.ds(start, CHUNK), :])
    root = jnp.sqrt(squares / (PARTS * CHUNK) + EPS)
    inverse = 1.0 / root
    return (q * inverse).astype(BF16), (k * inverse).astype(BF16), (v * inverse).astype(BF16), root


def start_of(me, k):
    return pl.multiple_of((me ^ k) * CHUNK, CHUNK)


def heads_down(wide):
    return jnp.concatenate([wide[:, h * HEAD : (h + 1) * HEAD] for h in range(HEADS)], axis=0)


def heads_across(tall):
    return jnp.concatenate([tall[h * ROWS : (h + 1) * ROWS] for h in range(HEADS)], axis=1)


def causal_scores(q, k):
    scores = dot(q, k, NT) * SCALE
    row = lax.broadcasted_iota(jnp.int32, scores.shape, 0) & (ROWS - 1)
    column = lax.broadcasted_iota(jnp.int32, scores.shape, 1)
    return jnp.where(row >= column, scores, F32(-1e30))


FORWARD, BACKWARD, STASH = (4, 1, 3), (3, 4, 1), (1, 3, 4)
SPREAD = (0, 4, 2, 6, 1, 5, 3, 7)


def hypercube_masks(order):
    masks = (0,)
    for step in order:
        masks += tuple(m ^ step for m in masks)
    return masks


def chunks_of(pieces):
    return [p[:, i : i + CHUNK] for p in pieces for i in range(0, p.shape[1], CHUNK)]


def starts_of(me, masks):
    return [start_of(me, m) for m in masks]


def forward_kernel(masks, place_ref, *refs):
    pieces, (gain, wq, wk, wv, attended) = refs[:-5], refs[-5:]
    starts = starts_of(place_ref[0], masks)
    q, k, v, _ = project(chunks_of(pieces), starts, gain, wq, wk, wv)
    scores = causal_scores(heads_down(q), k)
    weights = jnp.exp(scores - jnp.max(scores, axis=1, keepdims=True))
    total = jnp.sum(weights, axis=1, keepdims=True)
    mixed = dot(weights.astype(BF16), v) / total
    attended[...] = heads_across(mixed).astype(BF16)


def scatter_starts(me):
    return [start_of(me, j ^ half) for j in (2, 1, 3, 0) for half in (0, 4)]


def put_part(refs, i, part):
    ref, column = refs[i // 2], (i % 2) * CHUNK
    ref[:, column : column + CHUNK] = part.astype(ref.dtype)


def out_kernel(place_ref, attended, wo, p2, p1, p3, mine):
    for i, start in enumerate(scatter_starts(place_ref[0])):
        put_part((p2, p1, p3, mine), i, dot(attended[...], wo[:, pl.ds(start, CHUNK)]))


def forward_sum_kernel(tick, place_ref, mine, p2, p1, p3, x, edge, relayed, crossing, total):
    t = mine[...] + p2[...].astype(F32) + p1[...].astype(F32) + p3[...].astype(F32)
    own, other = t[:, :CHUNK], t[:, CHUNK:]
    own = own + x[:, :CHUNK].astype(F32)
    total[...] = own
    crossing[...] = other.astype(BF16)
    last = place_ref[2] == 1
    relayed[:, :CHUNK] = jnp.where(last, edge[tick].astype(F32), own).astype(BF16)
    relayed[:, CHUNK:] = jnp.where(last, 0.0, other).astype(BF16)


def keep(q, k, v, r, own, other, qkv, xhat, root):
    qkv[:, :CHUNK] = q
    qkv[:, CHUNK : CHUNK + KV] = k
    qkv[:, CHUNK + KV :] = v
    root[...] = jnp.broadcast_to(r, root.shape)
    xhat[:, :CHUNK] = own.astype(F32) / r
    xhat[:, CHUNK:] = other.astype(F32) / r


def recompute_near_kernel(masks, place_ref, *refs):
    pieces, (gain, wq, wk, wv, qkv, xhat, root) = refs[:-7], refs[-7:]
    chunks = chunks_of(pieces)
    starts = starts_of(place_ref[0], masks)
    q, k, v, r = project(chunks, starts, gain, wq, wk, wv)
    keep(q, k, v, r, chunks[masks.index(0)], chunks[masks.index(4)], qkv, xhat, root)


def recompute_far_kernel(place_ref, stash, gain, wq, wk, wv, qkv, xhat, root):
    me = place_ref[0]
    q, k, v, r = project(
        [stash[i] for i in range(PARTS)],
        [i * CHUNK for i in range(PARTS)],
        gain,
        wq,
        wk,
        wv,
    )
    keep(q, k, v, r, stash[me], stash[me ^ 4], qkv, xhat, root)


def backward_kernel(masks, row, place_ref, *refs):
    pieces, (qkv, wo, d_qkv, stat) = refs[:-4], refs[-4:]
    qkv = qkv.at[row : row + ROWS]
    d_att = jnp.zeros((ROWS, CHUNK), F32)
    for chunk, start in zip(chunks_of(pieces), starts_of(place_ref[0], masks)):
        d_att += dot(chunk, wo[:, pl.ds(start, CHUNK)], NT)
    q = heads_down(qkv[:, :CHUNK])
    k = qkv[:, CHUNK : CHUNK + KV]
    v = qkv[:, CHUNK + KV :]
    d_out = heads_down(d_att).astype(BF16)
    scores = causal_scores(q, k)
    weights = jnp.exp(scores - jnp.max(scores, axis=1, keepdims=True))
    weights = weights / jnp.sum(weights, axis=1, keepdims=True)
    d_weights = dot(d_out, v, NT)
    centre = jnp.sum(d_weights * weights, axis=1, keepdims=True)
    d_scores = (weights * (d_weights - centre) * SCALE).astype(BF16)
    d_q = heads_across(dot(d_scores, k)).astype(BF16)
    d_k = dot(d_scores, q, TN).astype(BF16)
    d_v = dot(weights.astype(BF16), d_out, TN).astype(BF16)
    d_qkv[:, :CHUNK] = d_q
    d_qkv[:, CHUNK : CHUNK + KV] = d_k
    d_qkv[:, CHUNK + KV :] = d_v
    product = d_qkv[...].astype(F32) * qkv[...].astype(F32)
    stat[...] = jnp.broadcast_to(jnp.sum(product, axis=1, keepdims=True), stat.shape)


def pack_stat(s):
    high = s.astype(BF16).astype(F32)
    lane = lax.broadcasted_iota(jnp.int32, (ROWS, KV), 1)
    return jnp.where(lane == 0, high, s - high).astype(BF16)


def unpack_stat(packed):
    wide = packed.astype(F32)
    return wide[:, 0:1] + wide[:, 1:2]


def norm_cotangent_kernel(place_ref, d_qkv, stat, wq, wk, wv, p2, p1, p3, mine):
    packed = pack_stat(stat[:, :1])
    for p in (p2, p1, p3):
        p[:, 2 * CHUNK :] = packed
    d_q, d_k, d_v = d_qkv[:, :CHUNK], d_qkv[:, CHUNK : CHUNK + KV], d_qkv[:, CHUNK + KV :]
    for i, start in enumerate(scatter_starts(place_ref[0])):
        rows = pl.ds(start, CHUNK)
        part = dot(d_q, wq[rows, :], NT) + dot(d_k, wk[rows, :], NT) + dot(d_v, wv[rows, :], NT)
        put_part((p2, p1, p3, mine), i, part)


def backward_sum_kernel(
    tick, row, place_ref, mine, stat, p2, p1, p3, xhat, root, gain, c, edge, relayed, crossing, total, stat_out
):
    me = place_ref[0]
    t = mine[...]
    s = stat[:, :1]
    for p in (p2, p1, p3):
        t = t + p[:, : 2 * CHUNK].astype(F32)
        s = s + unpack_stat(p[:, 2 * CHUNK :])
    own, other = t[:, :CHUNK], t[:, CHUNK:]
    total[...] = own
    stat_out[...] = jnp.broadcast_to(s, stat_out.shape)
    crossing[:, :CHUNK] = other.astype(BF16)
    crossing[:, CHUNK:] = pack_stat(s)
    mean = s / (PARTS * CHUNK)
    rows = slice(row, row + ROWS)
    xhat = xhat[rows, :]
    inverse = 1.0 / root[rows, :1]
    near = (own * gain[:, pl.ds(start_of(me, 0), CHUNK)] - xhat[:, :CHUNK] * mean) * inverse
    far = (other * gain[:, pl.ds(start_of(me, 4), CHUNK)] - xhat[:, CHUNK:] * mean) * inverse
    near = near + c[:, :CHUNK].astype(F32)
    first = place_ref[1] == 1
    relayed[:, :CHUNK] = jnp.where(first, edge[tick].astype(F32), near).astype(BF16)
    relayed[:, CHUNK:] = jnp.where(first, 0.0, far).astype(BF16)


def merge_kernel(place_ref, straight, across, pair):
    for half in (0, CHUNK):
        other = across[:, CHUNK - half : 2 * CHUNK - half].astype(F32)
        total = straight[:, half : half + CHUNK].astype(F32) + other
        pair[:, half : half + CHUNK] = total.astype(BF16)


def swap(value, mask):
    return lax.ppermute(value, "mp", [(i, i ^ mask) for i in range(PARTS)])


def spread(pair):
    far = {j: swap(pair, j) for j in (2, 1, 3)}
    return [pair, far[2], far[1], far[3]]


def gather(mine, order):
    for step in order[:-1]:
        mine = jnp.concatenate([mine, swap(mine, step)], axis=1)
    return [mine, swap(mine, order[-1])]


def relay(payload, step, sections, me, after=()):
    def pairs(mask):
        return [
            (s * PARTS + i, (s + step) % sections * PARTS + (i ^ mask))
            for s in range(sections)
            for i in range(PARTS)
        ]

    straight = lax.ppermute(payload, ("section", "mp"), pairs(0))
    across = lax.ppermute(payload, ("section", "mp"), pairs(4))
    shape = jax.ShapeDtypeStruct((ROWS, 2 * CHUNK), BF16)
    return call(merge_kernel, [shape], [straight, across], me, after)[0]


def on_device(
    arriving,
    returning,
    entering,
    cot_entering,
    home_stash,
    spare_stash,
    evicted,
    norm_gain,
    query_weight_matrix,
    key_weight_matrix,
    value_weight_matrix,
    w_output,
):
    sections = lax.axis_size("section")
    section = lax.axis_index("section")
    place = lax.axis_index("mp")
    me = jnp.stack([place, section == 0, section == sections - 1]).astype(jnp.int32)
    gain = norm_gain
    gain_mine = lax.dynamic_slice_in_dim(norm_gain, place * CHUNK, CHUNK, 1)
    wq, wk, wv, wo = (
        query_weight_matrix[0],
        key_weight_matrix[0],
        value_weight_matrix[0],
        w_output[0],
    )
    mirror = [(sections - 1 - s, s) for s in range(sections // 2)]
    wide = lambda rows, columns, kind: jax.ShapeDtypeStruct((rows, columns), kind)
    rest = (TICKS - 1) * ROWS

    x_all = gather(arriving[0], FORWARD)
    c_all = gather(returning[0], BACKWARD)
    fetched_first = lax.ppermute(spare_stash[0, 0], "section", mirror)
    stash_first = jnp.where(evicted[0, 0] == 1, fetched_first, home_stash[0, 0])
    stash_all = gather(stash_first, STASH)
    spare_rest = jnp.where(evicted[0, 0] == 2, fetched_first, spare_stash[0, 1:])
    fetched_rest = lax.ppermute(spare_rest, "section", mirror)
    saved = []
    forward_totals, backward_totals, crossings = [], [], []
    before = [c_all[1], stash_all[1]]
    for tick in range(TICKS):
        final = tick + 1 == TICKS
        edge = min(tick, TICKS - 2)
        row = max(tick - 1, 0) * ROWS
        attended = call(
            functools.partial(forward_kernel, hypercube_masks(FORWARD) if tick == 0 else SPREAD),
            [wide(ROWS, CHUNK, BF16)],
            x_all + [gain],
            me,
            before,
            [wq, wk, wv],
        )[0]
        if tick == 0:
            home_rest = jnp.where(evicted[0, 0] == 2, attended, home_stash[0, 1:])
            stash_rest = jnp.where(evicted[0, 1:, None, None] == 1, fetched_rest, home_rest)
            full_rest = lax.all_gather(stash_rest.reshape(rest, CHUNK), "mp")
        p2, p1, p3, mine = call(
            out_kernel,
            [wide(ROWS, 2 * CHUNK, BF16)] * 3 + [wide(ROWS, 2 * CHUNK, F32)],
            [attended],
            me,
            (),
            [wo],
        )
        f_parts = [mine, swap(p2, 2), swap(p1, 1), swap(p3, 3)]
        if tick == 0:
            kept = call(
                functools.partial(recompute_near_kernel, hypercube_masks(STASH)),
                [wide(ROWS, QKV, BF16), wide(ROWS, 2 * CHUNK, F32), wide(ROWS, KV, F32)],
                stash_all + [gain],
                me,
                [mine] + c_all[1:],
                [wq, wk, wv],
                )
            saved.append(kept)
        if tick == 1:
            far = call(
                recompute_far_kernel,
                [wide(rest, QKV, BF16), wide(rest, 2 * CHUNK, F32), wide(rest, KV, F32)],
                [full_rest, gain],
                me,
                [mine],
                [wq, wk, wv],
                )
            saved += [far] * (TICKS - 1)
        qkv, xhat, root = saved[tick]
        d_qkv, stat = call(
            functools.partial(
                backward_kernel, hypercube_masks(BACKWARD) if tick == 0 else SPREAD, row
            ),
            [wide(ROWS, QKV, BF16), wide(ROWS, KV, F32)],
            c_all + [qkv],
            me,
            [mine],
            [wo],
        )
        b2, b1, b3, b_mine = call(
            norm_cotangent_kernel,
            [wide(ROWS, 2 * CHUNK + KV, BF16)] * 3 + [wide(ROWS, 2 * CHUNK, F32)],
            [d_qkv, stat],
            me,
            (),
            [wq, wk, wv],
        )
        b_parts = [b_mine, stat, swap(b2, 2), swap(b1, 1), swap(b3, 3)]
        relayed, crossing, total = call(
            functools.partial(forward_sum_kernel, edge),
            [wide(ROWS, 2 * CHUNK, BF16), wide(ROWS, CHUNK, BF16), wide(ROWS, CHUNK, F32)],
            f_parts + [x_all[0], entering],
            me,
            [b_mine],
        )
        before = [crossing]
        if not final:
            x_all = spread(relay(relayed, 1, sections, me))
            before = [x_all[0]]
        forward_totals.append(total)
        crossings.append(crossing)

        c = c_all[0]
        relayed, crossing, total, stat = call(
            functools.partial(backward_sum_kernel, edge, row),
            [
                wide(ROWS, 2 * CHUNK, BF16),
                wide(ROWS, CHUNK + KV, BF16),
                wide(ROWS, CHUNK, F32),
                wide(ROWS, KV, F32),
            ],
            b_parts + [xhat, root, gain, c, cot_entering],
            me,
            before,
        )
        if not final:
            c_all = spread(relay(relayed, -1, sections, me, x_all[1:]))
            before = [c_all[0]]
        rows = slice(row, row + ROWS)
        backward_totals.append((total, stat, xhat[rows, :CHUNK], root[rows, :1], c[:, :CHUNK]))
        crossings.append(crossing)

    early = swap(jnp.concatenate(crossings[:-2], axis=1), 4)
    crossed = []
    for crossing in crossings[:-2]:
        crossed.append(early[:, : crossing.shape[1]])
        early = early[:, crossing.shape[1] :]
    crossed += [swap(crossing, 4) for crossing in crossings[-2:]]
    outputs, cots = [], []
    gain_total = jnp.zeros((1, CHUNK), F32)
    for tick in range(TICKS):
        forward, backward = crossed[2 * tick : 2 * tick + 2]
        outputs.append((forward_totals[tick] + forward.astype(F32)).astype(BF16))
        total, stat, xhat, root, c = backward_totals[tick]
        d_norm = total + backward[:, :CHUNK].astype(F32)
        mean = (stat[:, :1] + unpack_stat(backward[:, CHUNK:])) / (PARTS * CHUNK)
        back = c.astype(F32) + (d_norm * gain_mine - xhat * mean) / root
        cots.append(back.astype(BF16))
        gain_total = gain_total + jnp.sum(d_norm * xhat, axis=0, keepdims=True)
    gain_grad = gain_total + lax.ppermute(gain_total, "dp", [(0, 1), (1, 0)])
    return (jnp.stack(outputs)[None], jnp.stack(cots)[None], gain_grad)


def solution(mesh):
    placed = (
        P("section", "dp", "mp"),
        P("section", "dp", "mp"),
        P(None, "dp", "mp"),
        P(None, "dp", "mp"),
        P("section", None, "dp", "mp"),
        P("section", None, "dp", "mp"),
        P("section", None),
        P("section", None),
        P("section", None, "mp"),
        P("section", None, "mp"),
        P("section", None, "mp"),
        P("section", "mp", None),
    )
    return jax.shard_map(
        on_device,
        mesh=mesh,
        in_specs=placed,
        out_specs=(
            P("section", None, "dp", "mp"),
            P("section", None, "dp", "mp"),
            P("section", "mp"),
        ),
        check_vma=False,
    )
```

```python
import functools

import jax
import jax.numpy as jnp
from jax import lax
from jax.experimental import pallas as pl
from jax.experimental.pallas import tpu as pltpu
from jax.sharding import PartitionSpec as P

HEAD = 128
TICKS = 3
PARTS = 8
CHUNK = 512
ROWS = 128
KV = 128
HEADS = CHUNK // HEAD
QKV = CHUNK + 2 * KV
EPS = 1e-05
SCALE = HEAD**-0.5
F32 = jnp.float32
BF16 = jnp.bfloat16
NT = (((1,), (1,)), ((), ()))
TN = (((0,), (0,)), ((), ()))
VMEM_LIMIT = 48 * 2**20
VMEM = pl.BlockSpec(memory_space=pltpu.VMEM)
ANY = pl.BlockSpec(memory_space=pl.ANY)
SMEM = pl.BlockSpec(memory_space=pltpu.SMEM)


def call(kernel, outs, ins, me, after=(), weights=()):
    count = len(ins) + len(weights)

    name = getattr(kernel, "func", kernel).__name__

    def body(place_ref, *refs):
        kernel(place_ref, *refs[:count], *refs[count + len(after) :])

    return pl.pallas_call(
        body,
        out_shape=outs,
        in_specs=[SMEM] + [VMEM] * count + [ANY] * len(after),
        out_specs=[VMEM] * len(outs),
        compiler_params=pltpu.CompilerParams(vmem_limit_bytes=VMEM_LIMIT),
        cost_estimate=pl.CostEstimate(flops=1, bytes_accessed=1, transcendentals=0),
        name=name,
    )(me, *ins, *weights, *after)


def dot(a, b, dims=(((1,), (0,)), ((), ()))):
    return lax.dot_general(a, b, dims, preferred_element_type=F32)


def project(chunks, starts, gain, wq, wk, wv):
    rows = chunks[0].shape[0]
    squares = jnp.zeros((rows, 1), F32)
    q = jnp.zeros((rows, CHUNK), F32)
    k = jnp.zeros((rows, KV), F32)
    v = jnp.zeros((rows, KV), F32)
    for chunk, start in zip(chunks, starts):
        x = chunk.astype(F32)
        squares += jnp.sum(x * x, axis=1, keepdims=True)
        xg = (x * gain[:, pl.ds(start, CHUNK)]).astype(BF16)
        q += dot(xg, wq[pl.ds(start, CHUNK), :])
        k += dot(xg, wk[pl.ds(start, CHUNK), :])
        v += dot(xg, wv[pl.ds(start, CHUNK), :])
    root = jnp.sqrt(squares / (PARTS * CHUNK) + EPS)
    inverse = 1.0 / root
    return (q * inverse).astype(BF16), (k * inverse).astype(BF16), (v * inverse).astype(BF16), root


def start_of(me, k):
    return pl.multiple_of((me ^ k) * CHUNK, CHUNK)


def heads_down(wide):
    return jnp.concatenate([wide[:, h * HEAD : (h + 1) * HEAD] for h in range(HEADS)], axis=0)


def heads_across(tall):
    return jnp.concatenate([tall[h * ROWS : (h + 1) * ROWS] for h in range(HEADS)], axis=1)


def causal_scores(q, k):
    scores = dot(q, k, NT) * SCALE
    row = lax.broadcasted_iota(jnp.int32, scores.shape, 0) & (ROWS - 1)
    column = lax.broadcasted_iota(jnp.int32, scores.shape, 1)
    return jnp.where(row >= column, scores, F32(-1e30))


FORWARD, BACKWARD, STASH = (4, 1, 3), (3, 4, 1), (1, 3, 4)
SPREAD = (0, 4, 2, 6, 1, 5, 3, 7)


def hypercube_masks(order):
    masks = (0,)
    for step in order:
        masks += tuple(m ^ step for m in masks)
    return masks


def chunks_of(pieces):
    return [p[:, i : i + CHUNK] for p in pieces for i in range(0, p.shape[1], CHUNK)]


def starts_of(me, masks):
    return [start_of(me, m) for m in masks]


def forward_kernel(masks, place_ref, *refs):
    pieces, (gain, wq, wk, wv, attended) = refs[:-5], refs[-5:]
    starts = starts_of(place_ref[0], masks)
    q, k, v, _ = project(chunks_of(pieces), starts, gain, wq, wk, wv)
    scores = causal_scores(heads_down(q), k)
    weights = jnp.exp(scores - jnp.max(scores, axis=1, keepdims=True))
    total = jnp.sum(weights, axis=1, keepdims=True)
    mixed = dot(weights.astype(BF16), v) / total
    attended[...] = heads_across(mixed).astype(BF16)


def scatter_starts(me):
    return [start_of(me, j ^ half) for j in (2, 1, 3, 0) for half in (0, 4)]


def put_part(refs, i, part):
    ref, column = refs[i // 2], (i % 2) * CHUNK
    ref[:, column : column + CHUNK] = part.astype(ref.dtype)


def out_kernel(place_ref, attended, wo, p2, p1, p3, mine):
    for i, start in enumerate(scatter_starts(place_ref[0])):
        put_part((p2, p1, p3, mine), i, dot(attended[...], wo[:, pl.ds(start, CHUNK)]))


def forward_sum_kernel(tick, place_ref, mine, p2, p1, p3, x, edge, relayed, crossing, total):
    t = mine[...] + p2[...].astype(F32) + p1[...].astype(F32) + p3[...].astype(F32)
    own, other = t[:, :CHUNK], t[:, CHUNK:]
    own = own + x[:, :CHUNK].astype(F32)
    total[...] = own
    crossing[...] = other.astype(BF16)
    last = place_ref[2] == 1
    relayed[:, :CHUNK] = jnp.where(last, edge[tick].astype(F32), own).astype(BF16)
    relayed[:, CHUNK:] = jnp.where(last, 0.0, other).astype(BF16)


def keep(q, k, v, r, own, other, qkv, xhat, root):
    qkv[:, :CHUNK] = q
    qkv[:, CHUNK : CHUNK + KV] = k
    qkv[:, CHUNK + KV :] = v
    root[...] = jnp.broadcast_to(r, root.shape)
    xhat[:, :CHUNK] = own.astype(F32) / r
    xhat[:, CHUNK:] = other.astype(F32) / r


def recompute_near_kernel(masks, place_ref, *refs):
    pieces, (gain, wq, wk, wv, qkv, xhat, root) = refs[:-7], refs[-7:]
    chunks = chunks_of(pieces)
    starts = starts_of(place_ref[0], masks)
    q, k, v, r = project(chunks, starts, gain, wq, wk, wv)
    keep(q, k, v, r, chunks[masks.index(0)], chunks[masks.index(4)], qkv, xhat, root)


def recompute_far_kernel(place_ref, stash, gain, wq, wk, wv, qkv, xhat, root):
    me = place_ref[0]
    q, k, v, r = project(
        [stash[i] for i in range(PARTS)],
        [i * CHUNK for i in range(PARTS)],
        gain,
        wq,
        wk,
        wv,
    )
    keep(q, k, v, r, stash[me], stash[me ^ 4], qkv, xhat, root)


def backward_kernel(masks, row, place_ref, *refs):
    pieces, (qkv, wo, d_qkv, stat) = refs[:-4], refs[-4:]
    qkv = qkv.at[row : row + ROWS]
    d_att = jnp.zeros((ROWS, CHUNK), F32)
    for chunk, start in zip(chunks_of(pieces), starts_of(place_ref[0], masks)):
        d_att += dot(chunk, wo[:, pl.ds(start, CHUNK)], NT)
    q = heads_down(qkv[:, :CHUNK])
    k = qkv[:, CHUNK : CHUNK + KV]
    v = qkv[:, CHUNK + KV :]
    d_out = heads_down(d_att).astype(BF16)
    scores = causal_scores(q, k)
    weights = jnp.exp(scores - jnp.max(scores, axis=1, keepdims=True))
    weights = weights / jnp.sum(weights, axis=1, keepdims=True)
    d_weights = dot(d_out, v, NT)
    centre = jnp.sum(d_weights * weights, axis=1, keepdims=True)
    d_scores = (weights * (d_weights - centre) * SCALE).astype(BF16)
    d_q = heads_across(dot(d_scores, k)).astype(BF16)
    d_k = dot(d_scores, q, TN).astype(BF16)
    d_v = dot(weights.astype(BF16), d_out, TN).astype(BF16)
    d_qkv[:, :CHUNK] = d_q
    d_qkv[:, CHUNK : CHUNK + KV] = d_k
    d_qkv[:, CHUNK + KV :] = d_v
    product = d_qkv[...].astype(F32) * qkv[...].astype(F32)
    stat[...] = jnp.broadcast_to(jnp.sum(product, axis=1, keepdims=True), stat.shape)


def pack_stat(s):
    high = s.astype(BF16).astype(F32)
    lane = lax.broadcasted_iota(jnp.int32, (ROWS, KV), 1)
    return jnp.where(lane == 0, high, s - high).astype(BF16)


def unpack_stat(packed):
    wide = packed.astype(F32)
    return wide[:, 0:1] + wide[:, 1:2]


def norm_cotangent_kernel(place_ref, d_qkv, stat, wq, wk, wv, p2, p1, p3, mine):
    packed = pack_stat(stat[:, :1])
    for p in (p2, p1, p3):
        p[:, 2 * CHUNK :] = packed
    d_q, d_k, d_v = d_qkv[:, :CHUNK], d_qkv[:, CHUNK : CHUNK + KV], d_qkv[:, CHUNK + KV :]
    for i, start in enumerate(scatter_starts(place_ref[0])):
        rows = pl.ds(start, CHUNK)
        part = dot(d_q, wq[rows, :], NT) + dot(d_k, wk[rows, :], NT) + dot(d_v, wv[rows, :], NT)
        put_part((p2, p1, p3, mine), i, part)


def backward_sum_kernel(
    tick, row, place_ref, mine, stat, p2, p1, p3, xhat, root, gain, c, edge, relayed, crossing, total, stat_out, grads
):
    me = place_ref[0]
    t = mine[...]
    s = stat[:, :1]
    for p in (p2, p1, p3):
        t = t + p[:, : 2 * CHUNK].astype(F32)
        s = s + unpack_stat(p[:, 2 * CHUNK :])
    own, other = t[:, :CHUNK], t[:, CHUNK:]
    total[...] = own
    stat_out[...] = jnp.broadcast_to(s, stat_out.shape)
    crossing[:, :CHUNK] = other.astype(BF16)
    crossing[:, CHUNK:] = pack_stat(s)
    mean = s / (PARTS * CHUNK)
    rows = slice(row, row + ROWS)
    xhat = xhat[rows, :]
    inverse = 1.0 / root[rows, :1]
    near = (own * gain[:, pl.ds(start_of(me, 0), CHUNK)] - xhat[:, :CHUNK] * mean) * inverse
    far = (other * gain[:, pl.ds(start_of(me, 4), CHUNK)] - xhat[:, CHUNK:] * mean) * inverse
    near = near + c[:, :CHUNK].astype(F32)
    grads[0:1, :] = jnp.sum(own * xhat[:, :CHUNK], axis=0, keepdims=True)
    grads[1:2, :] = jnp.sum(other * xhat[:, CHUNK:], axis=0, keepdims=True)
    first = place_ref[1] == 1
    relayed[:, :CHUNK] = jnp.where(first, edge[tick].astype(F32), near).astype(BF16)
    relayed[:, CHUNK:] = jnp.where(first, 0.0, far).astype(BF16)


def merge_kernel(place_ref, straight, across, pair):
    for half in (0, CHUNK):
        other = across[:, CHUNK - half : 2 * CHUNK - half].astype(F32)
        total = straight[:, half : half + CHUNK].astype(F32) + other
        pair[:, half : half + CHUNK] = total.astype(BF16)


def finish_kernel(place_ref, *refs):
    forward, backward, stats, c_rows = (refs[i : i + TICKS] for i in range(0, 4 * TICKS, TICKS))
    early, forward_last, backward_last = refs[12:15]
    near_xhat, near_root, far_xhat, far_root, gain, outputs, cots = refs[15:]
    gain_mine = gain[:, pl.ds(start_of(place_ref[0], 0), CHUNK)]
    for tick in range(TICKS):
        if tick + 1 < TICKS:
            first = tick * (2 * CHUNK + KV)
            f = early[:, first : first + CHUNK]
            b = early[:, first + CHUNK : first + 2 * CHUNK + KV]
        else:
            f, b = forward_last[...], backward_last[...]
        if tick == 0:
            xhat, root = near_xhat[:, :CHUNK], near_root[:, :1]
        else:
            rows = slice((tick - 1) * ROWS, tick * ROWS)
            xhat, root = far_xhat[rows, :CHUNK], far_root[rows, :1]
        outputs[tick] = (forward[tick][...] + f.astype(F32)).astype(BF16)
        d_norm = backward[tick][...] + b[:, :CHUNK].astype(F32)
        mean = (stats[tick][:, :1] + unpack_stat(b[:, CHUNK:])) / (PARTS * CHUNK)
        change = (d_norm * gain_mine - xhat * mean) * (1.0 / root)
        cots[tick] = (c_rows[tick][:, :CHUNK].astype(F32) + change).astype(BF16)


def swap(value, mask):
    return lax.ppermute(value, "mp", [(i, i ^ mask) for i in range(PARTS)])


def spread(pair):
    far = {j: swap(pair, j) for j in (2, 1, 3)}
    return [pair, far[2], far[1], far[3]]


def gather(mine, order):
    for step in order[:-1]:
        mine = jnp.concatenate([mine, swap(mine, step)], axis=1)
    return [mine, swap(mine, order[-1])]


def relay(payload, step, sections, me, after=()):
    def pairs(mask):
        return [
            (s * PARTS + i, (s + step) % sections * PARTS + (i ^ mask))
            for s in range(sections)
            for i in range(PARTS)
        ]

    straight = lax.ppermute(payload, ("section", "mp"), pairs(0))
    across = lax.ppermute(payload, ("section", "mp"), pairs(4))
    shape = jax.ShapeDtypeStruct((ROWS, 2 * CHUNK), BF16)
    return call(merge_kernel, [shape], [straight, across], me, after)[0]


def on_device(
    arriving,
    returning,
    entering,
    cot_entering,
    home_stash,
    spare_stash,
    evicted,
    norm_gain,
    query_weight_matrix,
    key_weight_matrix,
    value_weight_matrix,
    w_output,
):
    sections = lax.axis_size("section")
    section = lax.axis_index("section")
    place = lax.axis_index("mp")
    me = jnp.stack([place, section == 0, section == sections - 1]).astype(jnp.int32)
    gain = norm_gain
    wq, wk, wv, wo = (
        query_weight_matrix[0],
        key_weight_matrix[0],
        value_weight_matrix[0],
        w_output[0],
    )
    mirror = [(sections - 1 - s, s) for s in range(sections // 2)]
    wide = lambda rows, columns, kind: jax.ShapeDtypeStruct((rows, columns), kind)
    rest = (TICKS - 1) * ROWS

    x_all = gather(arriving[0], FORWARD)
    c_all = gather(returning[0], BACKWARD)
    fetched_first = lax.ppermute(spare_stash[0, 0], "section", mirror)
    stash_first = jnp.where(evicted[0, 0] == 1, fetched_first, home_stash[0, 0])
    stash_all = gather(stash_first, STASH)
    spare_rest = jnp.where(evicted[0, 0] == 2, fetched_first, spare_stash[0, 1:])
    fetched_rest = lax.ppermute(spare_rest, "section", mirror)
    saved = []
    forward_totals, backward_totals, crossings = [], [], []
    stats, c_rows, gains = [], [], []
    before = [c_all[1], stash_all[1]]
    for tick in range(TICKS):
        final = tick + 1 == TICKS
        edge = min(tick, TICKS - 2)
        row = max(tick - 1, 0) * ROWS
        attended = call(
            functools.partial(forward_kernel, hypercube_masks(FORWARD) if tick == 0 else SPREAD),
            [wide(ROWS, CHUNK, BF16)],
            x_all + [gain],
            me,
            before,
            [wq, wk, wv],
        )[0]
        if tick == 0:
            home_rest = jnp.where(evicted[0, 0] == 2, attended, home_stash[0, 1:])
            stash_rest = jnp.where(evicted[0, 1:, None, None] == 1, fetched_rest, home_rest)
            full_rest = lax.all_gather(stash_rest.reshape(rest, CHUNK), "mp")
        p2, p1, p3, mine = call(
            out_kernel,
            [wide(ROWS, 2 * CHUNK, BF16)] * 3 + [wide(ROWS, 2 * CHUNK, F32)],
            [attended],
            me,
            (),
            [wo],
        )
        f_parts = [mine, swap(p2, 2), swap(p1, 1), swap(p3, 3)]
        if tick == 0:
            kept = call(
                functools.partial(recompute_near_kernel, hypercube_masks(STASH)),
                [wide(ROWS, QKV, BF16), wide(ROWS, 2 * CHUNK, F32), wide(ROWS, KV, F32)],
                stash_all + [gain],
                me,
                [mine] + c_all[1:],
                [wq, wk, wv],
                )
            saved.append(kept)
        if tick == 1:
            far = call(
                recompute_far_kernel,
                [wide(rest, QKV, BF16), wide(rest, 2 * CHUNK, F32), wide(rest, KV, F32)],
                [full_rest, gain],
                me,
                [mine],
                [wq, wk, wv],
                )
            saved += [far] * (TICKS - 1)
        qkv, xhat, root = saved[tick]
        d_qkv, stat = call(
            functools.partial(
                backward_kernel, hypercube_masks(BACKWARD) if tick == 0 else SPREAD, row
            ),
            [wide(ROWS, QKV, BF16), wide(ROWS, KV, F32)],
            c_all + [qkv],
            me,
            [mine],
            [wo],
        )
        b2, b1, b3, b_mine = call(
            norm_cotangent_kernel,
            [wide(ROWS, 2 * CHUNK + KV, BF16)] * 3 + [wide(ROWS, 2 * CHUNK, F32)],
            [d_qkv, stat],
            me,
            (),
            [wq, wk, wv],
        )
        b_parts = [b_mine, stat, swap(b2, 2), swap(b1, 1), swap(b3, 3)]
        relayed, crossing, total = call(
            functools.partial(forward_sum_kernel, edge),
            [wide(ROWS, 2 * CHUNK, BF16), wide(ROWS, CHUNK, BF16), wide(ROWS, CHUNK, F32)],
            f_parts + [x_all[0], entering],
            me,
            [b_mine],
        )
        before = [crossing]
        if not final:
            x_all = spread(relay(relayed, 1, sections, me))
            before = [x_all[0]]
        forward_totals.append(total)
        crossings.append(crossing)

        c = c_all[0]
        relayed, crossing, total, stat, grads = call(
            functools.partial(backward_sum_kernel, edge, row),
            [
                wide(ROWS, 2 * CHUNK, BF16),
                wide(ROWS, CHUNK + KV, BF16),
                wide(ROWS, CHUNK, F32),
                wide(ROWS, KV, F32),
                wide(2, CHUNK, F32),
            ],
            b_parts + [xhat, root, gain, c, cot_entering],
            me,
            before,
        )
        if not final:
            c_all = spread(relay(relayed, -1, sections, me, x_all[1:]))
            before = [c_all[0]]
        backward_totals.append(total)
        stats.append(stat)
        c_rows.append(c)
        gains.append(grads)
        crossings.append(crossing)

    early = swap(jnp.concatenate(crossings[:-2], axis=1), 4)
    grads = gains[0] + gains[1] + gains[2]
    own, other = grads[0:1], grads[1:2]
    both = [(i * 2 + d, (i ^ 4) * 2 + (d ^ 1)) for i in range(PARTS) for d in range(2)]
    here = own + swap(other, 4)
    there = lax.ppermute(own, "dp", [(0, 1), (1, 0)]) + lax.ppermute(other, ("mp", "dp"), both)
    outputs, cots = call(
        finish_kernel,
        [jax.ShapeDtypeStruct((TICKS, ROWS, CHUNK), BF16)] * 2,
        forward_totals
        + backward_totals
        + stats
        + c_rows
        + [early, swap(crossings[-2], 4), swap(crossings[-1], 4)]
        + [saved[0][1], saved[0][2], saved[1][1], saved[1][2], gain],
        me,
    )
    return (outputs[None], cots[None], here + there)


def solution(mesh):
    placed = (
        P("section", "dp", "mp"),
        P("section", "dp", "mp"),
        P(None, "dp", "mp"),
        P(None, "dp", "mp"),
        P("section", None, "dp", "mp"),
        P("section", None, "dp", "mp"),
        P("section", None),
        P("section", None),
        P("section", None, "mp"),
        P("section", None, "mp"),
        P("section", None, "mp"),
        P("section", "mp", None),
    )
    return jax.shard_map(
        on_device,
        mesh=mesh,
        in_specs=placed,
        out_specs=(
            P("section", None, "dp", "mp"),
            P("section", None, "dp", "mp"),
            P("section", "mp"),
        ),
        check_vma=False,
    )
```

```python
import functools

import jax
import jax.numpy as jnp
from jax import lax
from jax.experimental import pallas as pl
from jax.experimental.pallas import tpu as pltpu
from jax.sharding import PartitionSpec as P

HEAD = 128
TICKS = 3
PARTS = 8
CHUNK = 512
ROWS = 128
KV = 128
HEADS = CHUNK // HEAD
QKV = CHUNK + 2 * KV
EPS = 1e-05
SCALE = HEAD**-0.5
F32 = jnp.float32
BF16 = jnp.bfloat16
NT = (((1,), (1,)), ((), ()))
TN = (((0,), (0,)), ((), ()))
VMEM_LIMIT = 32 * 2**20
VMEM = pl.BlockSpec(memory_space=pltpu.VMEM)
ANY = pl.BlockSpec(memory_space=pl.ANY)
SMEM = pl.BlockSpec(memory_space=pltpu.SMEM)


def call(kernel, outs, ins, me, after=(), weights=()):
    count = len(ins) + len(weights)

    name = getattr(kernel, "func", kernel).__name__

    def body(place_ref, *refs):
        kernel(place_ref, *refs[:count], *refs[count + len(after) :])

    return pl.pallas_call(
        body,
        out_shape=outs,
        in_specs=[SMEM] + [VMEM] * count + [ANY] * len(after),
        out_specs=[VMEM] * len(outs),
        compiler_params=pltpu.CompilerParams(vmem_limit_bytes=VMEM_LIMIT),
        cost_estimate=pl.CostEstimate(flops=1, bytes_accessed=1, transcendentals=0),
        name=name,
    )(me, *ins, *weights, *after)


def dot(a, b, dims=(((1,), (0,)), ((), ()))):
    return lax.dot_general(a, b, dims, preferred_element_type=F32)


def project(chunks, starts, gain, wq, wk, wv):
    rows = chunks[0].shape[0]
    squares = jnp.zeros((rows, 1), F32)
    q = jnp.zeros((rows, CHUNK), F32)
    k = jnp.zeros((rows, KV), F32)
    v = jnp.zeros((rows, KV), F32)
    for chunk, start in zip(chunks, starts):
        x = chunk.astype(F32)
        squares += jnp.sum(x * x, axis=1, keepdims=True)
        xg = (x * gain[:, pl.ds(start, CHUNK)]).astype(BF16)
        q += dot(xg, wq[pl.ds(start, CHUNK), :])
        k += dot(xg, wk[pl.ds(start, CHUNK), :])
        v += dot(xg, wv[pl.ds(start, CHUNK), :])
    root = jnp.sqrt(squares / (PARTS * CHUNK) + EPS)
    inverse = 1.0 / root
    return (q * inverse).astype(BF16), (k * inverse).astype(BF16), (v * inverse).astype(BF16), root


def start_of(me, k):
    return pl.multiple_of((me ^ k) * CHUNK, CHUNK)


def heads_down(wide):
    return jnp.concatenate([wide[:, h * HEAD : (h + 1) * HEAD] for h in range(HEADS)], axis=0)


def heads_across(tall):
    return jnp.concatenate([tall[h * ROWS : (h + 1) * ROWS] for h in range(HEADS)], axis=1)


def causal_scores(q, k):
    scores = dot(q, k, NT) * SCALE
    row = lax.broadcasted_iota(jnp.int32, scores.shape, 0) & (ROWS - 1)
    column = lax.broadcasted_iota(jnp.int32, scores.shape, 1)
    return jnp.where(row >= column, scores, F32(-1e30))


FORWARD, BACKWARD, STASH = (4, 1, 3), (3, 4, 1), (1, 3, 4)
SPREAD = (0, 4, 2, 6, 1, 5, 3, 7)


def hypercube_masks(order):
    masks = (0,)
    for step in order:
        masks += tuple(m ^ step for m in masks)
    return masks


def chunks_of(pieces):
    return [p[:, i : i + CHUNK] for p in pieces for i in range(0, p.shape[1], CHUNK)]


def starts_of(me, masks):
    return [start_of(me, m) for m in masks]


def forward_kernel(masks, place_ref, *refs):
    pieces, (gain, wq, wk, wv, attended) = refs[:-5], refs[-5:]
    starts = starts_of(place_ref[0], masks)
    q, k, v, _ = project(chunks_of(pieces), starts, gain, wq, wk, wv)
    scores = causal_scores(heads_down(q), k)
    weights = jnp.exp(scores - jnp.max(scores, axis=1, keepdims=True))
    total = jnp.sum(weights, axis=1, keepdims=True)
    mixed = dot(weights.astype(BF16), v) / total
    attended[...] = heads_across(mixed).astype(BF16)


def scatter_starts(me):
    return [start_of(me, j ^ half) for j in (2, 1, 3, 0) for half in (0, 4)]


def put_part(refs, i, part):
    ref, column = refs[i // 2], (i % 2) * CHUNK
    ref[:, column : column + CHUNK] = part.astype(ref.dtype)


def out_kernel(place_ref, attended, wo, p2, p1, p3, mine):
    for i, start in enumerate(scatter_starts(place_ref[0])):
        put_part((p2, p1, p3, mine), i, dot(attended[...], wo[:, pl.ds(start, CHUNK)]))


def forward_sum_kernel(tick, place_ref, mine, p2, p1, p3, x, edge, relayed, crossing, total):
    t = mine[...] + p2[...].astype(F32) + p1[...].astype(F32) + p3[...].astype(F32)
    own, other = t[:, :CHUNK], t[:, CHUNK:]
    own = own + x[:, :CHUNK].astype(F32)
    total[...] = own
    crossing[...] = other.astype(BF16)
    last = place_ref[2] == 1
    relayed[:, :CHUNK] = jnp.where(last, edge[tick].astype(F32), own).astype(BF16)
    relayed[:, CHUNK:] = jnp.where(last, 0.0, other).astype(BF16)


def keep(q, k, v, r, own, other, qkv, xhat, root):
    qkv[:, :CHUNK] = q
    qkv[:, CHUNK : CHUNK + KV] = k
    qkv[:, CHUNK + KV :] = v
    root[...] = jnp.broadcast_to(r, root.shape)
    xhat[:, :CHUNK] = own.astype(F32) / r
    xhat[:, CHUNK:] = other.astype(F32) / r


def recompute_near_kernel(masks, place_ref, *refs):
    pieces, (gain, wq, wk, wv, qkv, xhat, root) = refs[:-7], refs[-7:]
    chunks = chunks_of(pieces)
    starts = starts_of(place_ref[0], masks)
    q, k, v, r = project(chunks, starts, gain, wq, wk, wv)
    keep(q, k, v, r, chunks[masks.index(0)], chunks[masks.index(4)], qkv, xhat, root)


def recompute_far_kernel(place_ref, stash, gain, wq, wk, wv, qkv, xhat, root):
    me = place_ref[0]
    q, k, v, r = project(
        [stash[i] for i in range(PARTS)],
        [i * CHUNK for i in range(PARTS)],
        gain,
        wq,
        wk,
        wv,
    )
    keep(q, k, v, r, stash[me], stash[me ^ 4], qkv, xhat, root)


def backward_kernel(masks, row, place_ref, *refs):
    pieces, (qkv, wo, d_qkv, stat) = refs[:-4], refs[-4:]
    qkv = qkv.at[row : row + ROWS]
    d_att = jnp.zeros((ROWS, CHUNK), F32)
    for chunk, start in zip(chunks_of(pieces), starts_of(place_ref[0], masks)):
        d_att += dot(chunk, wo[:, pl.ds(start, CHUNK)], NT)
    q = heads_down(qkv[:, :CHUNK])
    k = qkv[:, CHUNK : CHUNK + KV]
    v = qkv[:, CHUNK + KV :]
    d_out = heads_down(d_att).astype(BF16)
    scores = causal_scores(q, k)
    weights = jnp.exp(scores - jnp.max(scores, axis=1, keepdims=True))
    weights = weights / jnp.sum(weights, axis=1, keepdims=True)
    d_weights = dot(d_out, v, NT)
    centre = jnp.sum(d_weights * weights, axis=1, keepdims=True)
    d_scores = (weights * (d_weights - centre) * SCALE).astype(BF16)
    d_q = heads_across(dot(d_scores, k)).astype(BF16)
    d_k = dot(d_scores, q, TN).astype(BF16)
    d_v = dot(weights.astype(BF16), d_out, TN).astype(BF16)
    d_qkv[:, :CHUNK] = d_q
    d_qkv[:, CHUNK : CHUNK + KV] = d_k
    d_qkv[:, CHUNK + KV :] = d_v
    product = d_qkv[...].astype(F32) * qkv[...].astype(F32)
    stat[...] = jnp.broadcast_to(jnp.sum(product, axis=1, keepdims=True), stat.shape)


def pack_stat(s):
    high = s.astype(BF16).astype(F32)
    lane = lax.broadcasted_iota(jnp.int32, (ROWS, KV), 1)
    return jnp.where(lane == 0, high, s - high).astype(BF16)


def unpack_stat(packed):
    wide = packed.astype(F32)
    return wide[:, 0:1] + wide[:, 1:2]


def norm_cotangent_kernel(place_ref, d_qkv, stat, wq, wk, wv, p2, p1, p3, mine):
    packed = pack_stat(stat[:, :1])
    for p in (p2, p1, p3):
        p[:, 2 * CHUNK :] = packed
    d_q, d_k, d_v = d_qkv[:, :CHUNK], d_qkv[:, CHUNK : CHUNK + KV], d_qkv[:, CHUNK + KV :]
    for i, start in enumerate(scatter_starts(place_ref[0])):
        rows = pl.ds(start, CHUNK)
        part = dot(d_q, wq[rows, :], NT) + dot(d_k, wk[rows, :], NT) + dot(d_v, wv[rows, :], NT)
        put_part((p2, p1, p3, mine), i, part)


def backward_sum_kernel(
    tick, row, place_ref, mine, stat, p2, p1, p3, xhat, root, gain, c, edge, relayed, crossing, total, stat_out, grads
):
    me = place_ref[0]
    t = mine[...]
    s = stat[:, :1]
    for p in (p2, p1, p3):
        t = t + p[:, : 2 * CHUNK].astype(F32)
        s = s + unpack_stat(p[:, 2 * CHUNK :])
    own, other = t[:, :CHUNK], t[:, CHUNK:]
    total[...] = own
    stat_out[...] = jnp.broadcast_to(s, stat_out.shape)
    crossing[:, :CHUNK] = other.astype(BF16)
    crossing[:, CHUNK:] = pack_stat(s)
    mean = s / (PARTS * CHUNK)
    rows = slice(row, row + ROWS)
    xhat = xhat[rows, :]
    inverse = 1.0 / root[rows, :1]
    near = (own * gain[:, pl.ds(start_of(me, 0), CHUNK)] - xhat[:, :CHUNK] * mean) * inverse
    far = (other * gain[:, pl.ds(start_of(me, 4), CHUNK)] - xhat[:, CHUNK:] * mean) * inverse
    near = near + c[:, :CHUNK].astype(F32)
    grads[0:1, :] = jnp.sum(own * xhat[:, :CHUNK], axis=0, keepdims=True)
    grads[1:2, :] = jnp.sum(other * xhat[:, CHUNK:], axis=0, keepdims=True)
    first = place_ref[1] == 1
    relayed[:, :CHUNK] = jnp.where(first, edge[tick].astype(F32), near).astype(BF16)
    relayed[:, CHUNK:] = jnp.where(first, 0.0, far).astype(BF16)


def merge_kernel(place_ref, straight, across, pair):
    for half in (0, CHUNK):
        other = across[:, CHUNK - half : 2 * CHUNK - half].astype(F32)
        total = straight[:, half : half + CHUNK].astype(F32) + other
        pair[:, half : half + CHUNK] = total.astype(BF16)


def finish_kernel(place_ref, *refs):
    forward, backward, stats, c_rows = (refs[i : i + TICKS] for i in range(0, 4 * TICKS, TICKS))
    early, forward_last, backward_last = refs[12:15]
    near_xhat, near_root, far_xhat, far_root, gain, outputs, cots = refs[15:]
    gain_mine = gain[:, pl.ds(start_of(place_ref[0], 0), CHUNK)]
    for tick in range(TICKS):
        if tick + 1 < TICKS:
            first = tick * (2 * CHUNK + KV)
            f = early[:, first : first + CHUNK]
            b = early[:, first + CHUNK : first + 2 * CHUNK + KV]
        else:
            f, b = forward_last[...], backward_last[...]
        if tick == 0:
            xhat, root = near_xhat[:, :CHUNK], near_root[:, :1]
        else:
            rows = slice((tick - 1) * ROWS, tick * ROWS)
            xhat, root = far_xhat[rows, :CHUNK], far_root[rows, :1]
        outputs[tick] = (forward[tick][...] + f.astype(F32)).astype(BF16)
        d_norm = backward[tick][...] + b[:, :CHUNK].astype(F32)
        mean = (stats[tick][:, :1] + unpack_stat(b[:, CHUNK:])) / (PARTS * CHUNK)
        change = (d_norm * gain_mine - xhat * mean) * (1.0 / root)
        cots[tick] = (c_rows[tick][:, :CHUNK].astype(F32) + change).astype(BF16)


def swap(value, mask):
    return lax.ppermute(value, "mp", [(i, i ^ mask) for i in range(PARTS)])


def spread(pair):
    far = {j: swap(pair, j) for j in (2, 1, 3)}
    return [pair, far[2], far[1], far[3]]


def gather(mine, order):
    for step in order[:-1]:
        mine = jnp.concatenate([mine, swap(mine, step)], axis=1)
    return [mine, swap(mine, order[-1])]


def relay(payload, step, sections, me, after=()):
    def pairs(mask):
        return [
            (s * PARTS + i, (s + step) % sections * PARTS + (i ^ mask))
            for s in range(sections)
            for i in range(PARTS)
        ]

    straight = lax.ppermute(payload, ("section", "mp"), pairs(0))
    across = lax.ppermute(payload, ("section", "mp"), pairs(4))
    shape = jax.ShapeDtypeStruct((ROWS, 2 * CHUNK), BF16)
    return call(merge_kernel, [shape], [straight, across], me, after)[0]


def on_device(
    arriving,
    returning,
    entering,
    cot_entering,
    home_stash,
    spare_stash,
    evicted,
    norm_gain,
    query_weight_matrix,
    key_weight_matrix,
    value_weight_matrix,
    w_output,
):
    sections = lax.axis_size("section")
    section = lax.axis_index("section")
    place = lax.axis_index("mp")
    me = jnp.stack([place, section == 0, section == sections - 1]).astype(jnp.int32)
    gain = norm_gain
    wq, wk, wv, wo = (
        query_weight_matrix[0],
        key_weight_matrix[0],
        value_weight_matrix[0],
        w_output[0],
    )
    mirror = [(sections - 1 - s, s) for s in range(sections // 2)]
    wide = lambda rows, columns, kind: jax.ShapeDtypeStruct((rows, columns), kind)
    rest = (TICKS - 1) * ROWS

    x_all = gather(arriving[0], FORWARD)
    c_all = gather(returning[0], BACKWARD)
    fetched_first = lax.ppermute(spare_stash[0, 0], "section", mirror)
    stash_first = jnp.where(evicted[0, 0] == 1, fetched_first, home_stash[0, 0])
    stash_all = gather(stash_first, STASH)
    spare_rest = jnp.where(evicted[0, 0] == 2, fetched_first, spare_stash[0, 1:])
    fetched_rest = lax.ppermute(spare_rest, "section", mirror)
    saved = []
    forward_totals, backward_totals, crossings = [], [], []
    stats, c_rows, gains = [], [], []
    before = [c_all[1], stash_all[1]]
    for tick in range(TICKS):
        final = tick + 1 == TICKS
        edge = min(tick, TICKS - 2)
        row = max(tick - 1, 0) * ROWS
        attended = call(
            functools.partial(forward_kernel, hypercube_masks(FORWARD) if tick == 0 else SPREAD),
            [wide(ROWS, CHUNK, BF16)],
            x_all + [gain],
            me,
            before,
            [wq, wk, wv],
        )[0]
        if tick == 0:
            home_rest = jnp.where(evicted[0, 0] == 2, attended, home_stash[0, 1:])
            stash_rest = jnp.where(evicted[0, 1:, None, None] == 1, fetched_rest, home_rest)
            full_rest = lax.all_gather(stash_rest.reshape(rest, CHUNK), "mp")
        p2, p1, p3, mine = call(
            out_kernel,
            [wide(ROWS, 2 * CHUNK, BF16)] * 3 + [wide(ROWS, 2 * CHUNK, F32)],
            [attended],
            me,
            (),
            [wo],
        )
        f_parts = [mine, swap(p2, 2), swap(p1, 1), swap(p3, 3)]
        if tick == 0:
            kept = call(
                functools.partial(recompute_near_kernel, hypercube_masks(STASH)),
                [wide(ROWS, QKV, BF16), wide(ROWS, 2 * CHUNK, F32), wide(ROWS, KV, F32)],
                stash_all + [gain],
                me,
                [mine] + c_all[1:],
                [wq, wk, wv],
                )
            saved.append(kept)
        if tick == 1:
            far = call(
                recompute_far_kernel,
                [wide(rest, QKV, BF16), wide(rest, 2 * CHUNK, F32), wide(rest, KV, F32)],
                [full_rest, gain],
                me,
                [mine],
                [wq, wk, wv],
                )
            saved += [far] * (TICKS - 1)
        qkv, xhat, root = saved[tick]
        d_qkv, stat = call(
            functools.partial(
                backward_kernel, hypercube_masks(BACKWARD) if tick == 0 else SPREAD, row
            ),
            [wide(ROWS, QKV, BF16), wide(ROWS, KV, F32)],
            c_all + [qkv],
            me,
            [mine],
            [wo],
        )
        b2, b1, b3, b_mine = call(
            norm_cotangent_kernel,
            [wide(ROWS, 2 * CHUNK + KV, BF16)] * 3 + [wide(ROWS, 2 * CHUNK, F32)],
            [d_qkv, stat],
            me,
            (),
            [wq, wk, wv],
        )
        b_parts = [b_mine, stat, swap(b2, 2), swap(b1, 1), swap(b3, 3)]
        relayed, crossing, total = call(
            functools.partial(forward_sum_kernel, edge),
            [wide(ROWS, 2 * CHUNK, BF16), wide(ROWS, CHUNK, BF16), wide(ROWS, CHUNK, F32)],
            f_parts + [x_all[0], entering],
            me,
            [b_mine],
        )
        before = [crossing]
        if not final:
            x_all = spread(relay(relayed, 1, sections, me))
            before = [x_all[0]]
        forward_totals.append(total)
        crossings.append(crossing)

        c = c_all[0]
        relayed, crossing, total, stat, grads = call(
            functools.partial(backward_sum_kernel, edge, row),
            [
                wide(ROWS, 2 * CHUNK, BF16),
                wide(ROWS, CHUNK + KV, BF16),
                wide(ROWS, CHUNK, F32),
                wide(ROWS, KV, F32),
                wide(2, CHUNK, F32),
            ],
            b_parts + [xhat, root, gain, c, cot_entering],
            me,
            before,
        )
        if not final:
            c_all = spread(relay(relayed, -1, sections, me, x_all[1:]))
            before = [c_all[0]]
        backward_totals.append(total)
        stats.append(stat)
        c_rows.append(c)
        gains.append(grads)
        crossings.append(crossing)

    early = swap(jnp.concatenate(crossings[:-2], axis=1), 4)
    grads = gains[0] + gains[1] + gains[2]
    own, other = grads[0:1], grads[1:2]
    both = [(i * 2 + d, (i ^ 4) * 2 + (d ^ 1)) for i in range(PARTS) for d in range(2)]
    here = own + swap(other, 4)
    there = lax.ppermute(own, "dp", [(0, 1), (1, 0)]) + lax.ppermute(other, ("mp", "dp"), both)
    outputs, cots = call(
        finish_kernel,
        [jax.ShapeDtypeStruct((TICKS, ROWS, CHUNK), BF16)] * 2,
        forward_totals
        + backward_totals
        + stats
        + c_rows
        + [early, swap(crossings[-2], 4), swap(crossings[-1], 4)]
        + [saved[0][1], saved[0][2], saved[1][1], saved[1][2], gain],
        me,
    )
    return (outputs[None], cots[None], here + there)


def solution(mesh):
    placed = (
        P("section", "dp", "mp"),
        P("section", "dp", "mp"),
        P(None, "dp", "mp"),
        P(None, "dp", "mp"),
        P("section", None, "dp", "mp"),
        P("section", None, "dp", "mp"),
        P("section", None),
        P("section", None),
        P("section", None, "mp"),
        P("section", None, "mp"),
        P("section", None, "mp"),
        P("section", "mp", None),
    )
    return jax.shard_map(
        on_device,
        mesh=mesh,
        in_specs=placed,
        out_specs=(
            P("section", None, "dp", "mp"),
            P("section", None, "dp", "mp"),
            P("section", "mp"),
        ),
        check_vma=False,
    )
```
